32 devices in a mesh: dp: 8 (over z, core), mp: 4 (over y, x).
Axes of the slice: x: 2, y: 2, z: 4, core: 2. Of those that a mesh axis runs over, the one named last changes fastest.
Arguments:
- tokens: bfloat16 [8192, 2048], P(('dp', 'mp')), may hold values from -6 to 6
- cotangent: bfloat16 [8192, 2048], P(('dp', 'mp')), may hold values from -6 to 6
- domain: int32 [8], P('dp'), may hold values from 0 to 3
- query_weight: bfloat16 [2048, 2048], P(('dp', 'mp')), may hold values from -0.125 to 0.125
- key_weight: bfloat16 [2048, 2048], P(('dp', 'mp')), may hold values from -0.125 to 0.125
- value_weight: bfloat16 [2048, 4096], P(('dp', 'mp')), may hold values from -0.125 to 0.125
- gate_weight: bfloat16 [2048, 4096], P(('dp', 'mp')), may hold values from -0.125 to 0.125
- output_weight: bfloat16 [4096, 2048], P(('dp', 'mp')), may hold values from -0.1875 to 0.1875
- retention_gain: bfloat16 [2048], P(('dp', 'mp')), may hold values from 0.099609375 to 1.8984375
- retention_bias: bfloat16 [2048], P(('dp', 'mp')), may hold values from -2 to 2
- feedfwd_gain: bfloat16 [2048], P(('dp', 'mp')), may hold values from 0.099609375 to 1.8984375
- feedfwd_bias: bfloat16 [2048], P(('dp', 'mp')), may hold values from -2 to 2
- up_weight: bfloat16 [2048, 4096], P('dp', 'mp'), may hold values from -0.125 to 0.125
- down_weight: bfloat16 [4096, 2048], P('mp', 'dp'), may hold values from -0.1875 to 0.1875
Outputs:
- outputs: bfloat16 [8192, 2048], P(('dp', 'mp'))
- tokens_grad: bfloat16 [8192, 2048], P(('dp', 'mp'))
- query_grad: float32 [2048, 2048], P(('dp', 'mp'))
- key_grad: float32 [2048, 2048], P(('dp', 'mp'))
- value_grad: float32 [2048, 4096], P(('dp', 'mp'))
- gate_grad: float32 [2048, 4096], P(('dp', 'mp'))
- output_grad: float32 [4096, 2048], P(('dp', 'mp'))
- retgain_grad: float32 [2048], P(('dp', 'mp'))
- retbias_grad: float32 [2048], P(('dp', 'mp'))
- ffngain_grad: float32 [2048], P(('dp', 'mp'))
- ffnbias_grad: float32 [2048], P(('dp', 'mp'))
- up_grad: float32 [2048, 4096], P('dp', 'mp')
- down_grad: float32 [4096, 2048], P('mp', 'dp')
The draws below stay inside these ranges and needn't reach their ends.
All inputs are finite; a program needn't handle non-finite values.
Results may differ from the reference program's by a relative error of at most 0.018.
Values may be sent and summed in bfloat16 or wider, within the bound.
No kernel may reach another device: no remote copies, remote signals or barrier semaphores. Data moves between devices by JAX's collectives and lax.ppermute only.
A program may use at most 448 MiB of HBM per device.

```python
import jax
import jax.numpy as jnp
from jax import lax

D = 2048
DV = 4096
FF = 4096
HEADS = 8
KHEAD = 256
VHEAD = 512
SPAN = 256
DOMAINS = 4
SEQ = 1024
NSEQ = 8
TOKENS = 8192


def place_ends(entries, stream_key, smallest, high):
    extent = entries.shape
    index_at = [jax.random.randint(jax.random.fold_in(stream_key, axis), (), 0, extent[axis]) for axis in range(len(extent))]
    entries = entries.at[tuple(index_at)].set(smallest)
    longest = extent.index(max(extent))
    index_at[longest] = (index_at[longest] + 1) % extent[longest]
    return entries.at[tuple(index_at)].set(high)


def with_spikes(entries, rng, source, target, blocks, factor):
    def block_of(axis_at):
        return (jnp.arange(entries.shape[axis_at]) // (entries.shape[axis_at] // blocks)).reshape((-1,) + (1,) * (entries.ndim - 1 - axis_at))

    first = jax.random.permutation(rng, blocks)[block_of(target)]
    other_side = (block_of(target) + blocks // 2) % blocks
    return jnp.where((block_of(source) == first) | (block_of(source) == other_side), factor * entries, entries)


def levels(rng, extent, cuts, least, largest):
    level, own = 1.0, jax.random.fold_in(rng, 6)
    for position, shards_of in cuts:
        draws = jnp.exp(jax.random.uniform(jax.random.fold_in(own, position), (shards_of,), jnp.float32, least / len(cuts), largest / len(cuts)))
        level = level * jnp.repeat(draws, extent[position] // shards_of).reshape([-1 if axis == position else 1 for axis in range(len(extent))])
    return level


def centred(stream_key, dims, deviation, bound, split=(), held_as=jnp.bfloat16):
    drawn = deviation * jax.random.normal(stream_key, dims, jnp.float32)
    if split:
        drawn = drawn * levels(stream_key, dims, split, -0.22, 0.18)
    return jnp.clip(drawn, -bound, bound).astype(held_as)


def noise_with(key, dims, scale, most, cuts, heavy, kind=jnp.bfloat16):
    values = scale * jax.random.normal(key, dims, jnp.float32)
    if cuts:
        values = values * levels(key, dims, cuts, -0.22, 0.18)
    return jnp.clip(with_spikes(values, jax.random.fold_in(key, 3), *heavy), -most, most).astype(kind)


def setup_inputs(seed: int = 0) -> dict:
    key_list = jax.random.split(jax.random.key(seed), 15)
    tokens = noise_with(key_list[0], (TOKENS, D), 1.0, 6.0, ((0, 32),), (0, 1, 32, 2.75))
    cotangent = centred(key_list[1], (TOKENS, D), 1.0, 6.0, ((0, 32),))
    domain = place_ends(jax.random.randint(key_list[2], (NSEQ,), 0, DOMAINS), jax.random.fold_in(key_list[2], 1), 0, DOMAINS - 1).astype(jnp.int32)
    query_weight = centred(key_list[3], (D, D), D ** -0.5, 0.125, ((0, 32),))
    key_weight = centred(key_list[4], (D, D), D ** -0.5, 0.125, ((0, 32),))
    value_weight = centred(key_list[5], (D, DV), D ** -0.5, 0.125, ((0, 32),))
    gate_weight = centred(key_list[6], (D, DV), D ** -0.5, 0.125, ((0, 32),))
    output_weight = centred(key_list[7], (DV, D), (DV // 4) ** -0.5, 0.1875, ((0, 32),))
    retention_gain = jnp.clip(1.0 + 0.18 * jax.random.normal(key_list[8], (D,), jnp.float32), 0.099609375, 1.8984375).astype(jnp.bfloat16)
    retention_bias = centred(key_list[9], (D,), 0.3, 2.0, ((0, 32),))
    feedfwd_gain = jnp.clip(1.0 + 0.18 * jax.random.normal(key_list[10], (D,), jnp.float32), 0.099609375, 1.8984375).astype(jnp.bfloat16)
    feedfwd_bias = centred(key_list[11], (D,), 0.3, 2.0, ((0, 32),))
    up_weight = centred(key_list[12], (D, FF), D ** -0.5, 0.125, ((0, 8), (1, 4)))
    down_weight = centred(key_list[13], (FF, D), (FF // 4) ** -0.5, 0.1875, ((0, 4), (1, 8)))
    return {"tokens": tokens, "cotangent": cotangent, "domain": domain, "query_weight": query_weight, "key_weight": key_weight, "value_weight": value_weight, "gate_weight": gate_weight, "output_weight": output_weight, "retention_gain": retention_gain, "retention_bias": retention_bias, "feedfwd_gain": feedfwd_gain, "feedfwd_bias": feedfwd_bias, "up_weight": up_weight, "down_weight": down_weight}


EPSILON = 1e-05

@jax.custom_vjp
def reduced_precision(v):
    return lax.optimization_barrier(v.astype(jnp.bfloat16)).astype(jnp.float32)

@jax.custom_vjp
def reduced_precision_backward(v):
    return v

def low_keep(v):
    return (reduced_precision(v), None)

def low_pass(kept, grad):
    return (grad,)

def back_keep(v):
    return (v, None)

def back_low(kept, grad):
    return (reduced_precision(grad),)
reduced_precision.defvjp(low_keep, low_pass)
reduced_precision_backward.defvjp(back_keep, back_low)

def matmul(left, right):
    return jnp.dot(left, right, precision=lax.Precision.HIGHEST)

def layer_norm(values, gain, bias):
    center = values - lax.optimization_barrier(jnp.mean(values, axis=-1, keepdims=True))
    factor = lax.rsqrt(lax.optimization_barrier(jnp.mean(center * center, axis=-1, keepdims=True)) + EPSILON)
    return center * factor * gain + bias

def group_norm(values):
    center = values - lax.optimization_barrier(jnp.mean(values, axis=-1, keepdims=True))
    return center * lax.rsqrt(lax.optimization_barrier(jnp.mean(center * center, axis=-1, keepdims=True)) + EPSILON)

def decay_logs(heads):
    return jnp.log1p(-jnp.exp2(-5.0 - jnp.arange(heads, dtype=jnp.float32)))

def rotation_tables(start, count, width):
    freq = 10000.0 ** (-2.0 * jnp.arange(width // 2, dtype=jnp.float32) / width)
    places = (start + jnp.arange(count, dtype=jnp.int32)).astype(jnp.float32)
    angle = places[:, None] * freq[None, :]
    return (jnp.cos(angle)[:, None, :], jnp.sin(angle)[:, None, :])

def rotate(values, cosine, sine):
    half = values.shape[-1] // 2
    first = values[..., :half]
    second = values[..., half:]
    return jnp.concatenate([first * cosine - second * sine, first * sine + second * cosine], axis=-1)

def retention(queries, keys, values):
    logs = decay_logs(HEADS)
    places = jnp.arange(SPAN, dtype=jnp.float32)
    spacing = places[:, None] - places[None, :]
    inner_decay = jnp.where(spacing[None] >= 0, jnp.exp(jnp.maximum(spacing, 0.0)[None] * logs[:, None, None]), 0.0)
    position_decay = jnp.exp(places[:, None] * logs[None, :])[:, :, None]
    key_decay = jnp.exp((SPAN - places)[:, None] * logs[None, :])[:, :, None]
    block_decay = jnp.exp(SPAN * logs)
    blocks = SEQ // SPAN

    def block_step(retention_state, piece):
        query_tile_rows, key_block, value_tile_rows = piece
        scores = reduced_precision_backward(jnp.einsum('nhk,mhk->hnm', query_tile_rows, key_block, precision=lax.Precision.HIGHEST))
        weights = reduced_precision(scores * inner_decay)
        inner = reduced_precision_backward(jnp.einsum('hnm,mhv->nhv', weights, value_tile_rows, precision=lax.Precision.HIGHEST))
        carried_state = reduced_precision_backward(jnp.einsum('zxd,xdg->zxg', query_tile_rows, reduced_precision(retention_state), precision=lax.Precision.HIGHEST)) * position_decay
        key_decayed = reduced_precision(key_block * key_decay)
        intra_block_output = reduced_precision_backward(jnp.einsum('jxb,jxy->xby', key_decayed, value_tile_rows, precision=lax.Precision.HIGHEST))
        return (retention_state * block_decay[:, None, None] + intra_block_output, inner + carried_state)
    zero = jnp.zeros((HEADS, KHEAD, VHEAD), jnp.float32)
    pieces = (queries.reshape(blocks, SPAN, HEADS, KHEAD), keys.reshape(blocks, SPAN, HEADS, KHEAD), values.reshape(blocks, SPAN, HEADS, VHEAD))
    _, result = lax.scan(jax.checkpoint(block_step), zero, pieces)
    return result.reshape(SEQ, HEADS, VHEAD)

def forward(sequence, params):
    w_query, w_key, w_value, w_gate, w_output, gain_one, bias_one, gain_two, bias_two, w_up, w_down = params
    normed_one = reduced_precision(layer_norm(sequence, gain_one, bias_one))
    query_pre = reduced_precision_backward(matmul(normed_one, w_query))
    key_pre = reduced_precision_backward(matmul(normed_one, w_key))
    value_pre = reduced_precision_backward(matmul(normed_one, w_value))
    gate_pre = reduced_precision_backward(matmul(normed_one, w_gate))
    cosine, sine = rotation_tables(0, SEQ, KHEAD)
    queries = reduced_precision(rotate(query_pre.reshape(SEQ, HEADS, KHEAD), cosine, sine))
    keys = reduced_precision(rotate(key_pre.reshape(SEQ, HEADS, KHEAD), cosine, sine))
    values = reduced_precision(value_pre).reshape(SEQ, HEADS, VHEAD)
    grouped = group_norm(retention(queries, keys, values)).reshape(SEQ, DV)
    gated = reduced_precision(gate_pre * jax.nn.sigmoid(gate_pre) * grouped)
    middle = sequence + reduced_precision_backward(matmul(gated, w_output))
    normed_two = reduced_precision(layer_norm(middle, gain_two, bias_two))
    hidden = reduced_precision(jax.nn.gelu(reduced_precision_backward(matmul(normed_two, w_up))))
    return middle + reduced_precision_backward(matmul(hidden, w_down))

def reference(tokens, cotangent, domain, query_weight, key_weight, value_weight, gate_weight, output_weight, retention_gain, retention_bias, feedfwd_gain, feedfwd_bias, up_weight, down_weight):
    params = tuple((w.astype(jnp.float32) for w in (query_weight, key_weight, value_weight, gate_weight, output_weight, retention_gain, retention_bias, feedfwd_gain, feedfwd_bias, up_weight, down_weight)))
    member = domain[:, None] == jnp.arange(DOMAINS, dtype=jnp.int32)[None, :]
    counts = lax.optimization_barrier(jnp.sum(member.astype(jnp.int32), axis=0)) * SEQ
    own_count = lax.optimization_barrier(jnp.sum(jnp.where(member, counts[None, :], 0), axis=1))
    row_scale = jnp.float32(TOKENS) / (DOMAINS * own_count.astype(jnp.float32))
    inputs = tokens.astype(jnp.float32).reshape(NSEQ, SEQ, D)
    grads_in = cotangent.astype(jnp.float32).reshape(NSEQ, SEQ, D) * row_scale[:, None, None]

    def one_sequence(totals, piece):
        sequence, seq_grad = piece
        result, pull = jax.vjp(forward, sequence, params)
        input_grad, param_grads = pull(seq_grad)
        return (jax.tree.map(jnp.add, totals, param_grads), (result, input_grad))
    start = tuple((jnp.zeros_like(w) for w in params))
    totals, (results, input_grads) = lax.scan(one_sequence, start, (inputs, grads_in))
    return (results.reshape(TOKENS, D).astype(jnp.bfloat16), input_grads.reshape(TOKENS, D).astype(jnp.bfloat16), totals[0], totals[1], totals[2], totals[3], totals[4], totals[5], totals[6], totals[7], totals[8], totals[9], totals[10])
```

```python
import functools

import jax
import jax.numpy as jnp
from jax import lax
from jax.experimental import pallas as pl
from jax.experimental.pallas import tpu as pltpu
from jax.sharding import PartitionSpec as P

D = 2048
DV = 4096
HEADS = 8
KHEAD = 256
VHEAD = 512
SPAN = 256
DOMAINS = 4


EPSILON = 1e-05
F32 = jnp.float32
BF16 = jnp.bfloat16


def layer_stats(values):
    center = values - jnp.mean(values, axis=-1, keepdims=True)
    factor = lax.rsqrt(jnp.mean(center * center, axis=-1, keepdims=True) + EPSILON)
    return (center * factor, factor)


def layer_back(grad, normal, factor):
    return factor * (
        grad
        - jnp.mean(grad, axis=-1, keepdims=True)
        - normal * jnp.mean(grad * normal, axis=-1, keepdims=True)
    )


def decay_logs(heads):
    return jnp.log1p(-jnp.exp2(-5.0 - jnp.arange(heads, dtype=jnp.float32)))


def rotation_tables(count, width):
    freq = 10000.0 ** (-2.0 * jnp.arange(width // 2, dtype=jnp.float32) / width)
    places = jnp.arange(count, dtype=jnp.int32).astype(jnp.float32)
    angle = places[:, None] * freq[None, :]
    return (jnp.cos(angle), jnp.sin(angle))


def dot(left, right):
    return jnp.dot(left, right, preferred_element_type=F32)


def contract_rows(left, right):
    return lax.dot_general(
        left, right, (((0,), (0,)), ((), ())), preferred_element_type=F32
    )


def contract_cols(left, right):
    return lax.dot_general(
        left, right, (((1,), (1,)), ((), ())), preferred_element_type=F32
    )


def rotate(values, cosine, sine):
    half = values.shape[-1] // 2
    first, second = values[:, :half], values[:, half:]
    return jnp.concatenate(
        [first * cosine - second * sine, first * sine + second * cosine], axis=-1
    )


def unrotate(values, cosine, sine):
    half = values.shape[-1] // 2
    first, second = values[:, :half], values[:, half:]
    return jnp.concatenate(
        [first * cosine + second * sine, second * cosine - first * sine], axis=-1
    )


def head_forward(h, heads, pre_ref, cosine, sine, inner_decay, place_decay, state_low):
    q_at, k_at = h * KHEAD, (heads + h) * KHEAD
    v_at, g_at = 2 * heads * KHEAD + h * VHEAD, 2 * heads * KHEAD + (heads + h) * VHEAD
    query = rotate(pre_ref[:, q_at : q_at + KHEAD], cosine, sine).astype(BF16)
    key = rotate(pre_ref[:, k_at : k_at + KHEAD], cosine, sine).astype(BF16)
    value = pre_ref[:, v_at : v_at + VHEAD].astype(BF16)
    gate = pre_ref[:, g_at : g_at + VHEAD]
    weights = (contract_cols(query, key) * inner_decay).astype(BF16)
    retained = dot(weights, value) + dot(query, state_low) * place_decay
    grouped, factor = layer_stats(retained)
    return query, key, value, gate, weights, grouped, factor


def retention_forward_kernel(
    heads, order_ref, block_ref, pre_ref, cos_ref, sin_ref, inner_ref, place_ref, key_ref,
    gated_ref, low_ref, state,
):
    @pl.when(pl.program_id(0) == 0)
    def _():
        state[...] = jnp.zeros_like(state)

    cosine, sine = cos_ref[...], sin_ref[...]
    for h in range(heads):
        before = state[h]
        state_low = before.astype(BF16)
        low_ref[0, h] = state_low
        query, key, value, gate, weights, grouped, factor = head_forward(
            h, heads, pre_ref, cosine, sine, inner_ref[h], place_ref[h], state_low
        )
        gated = gate * jax.nn.sigmoid(gate) * grouped
        gated_ref[:, h * VHEAD : (h + 1) * VHEAD] = gated.astype(BF16)
        key_scaled = (key.astype(F32) * key_ref[h]).astype(BF16)
        state[h] = before * block_ref[h] + contract_rows(key_scaled, value)


def retention_backward_kernel(
    heads, order_ref, block_ref, pre_ref, cos_ref, sin_ref, inner_ref, place_ref, key_ref,
    low_ref, grad_ref, out_ref, state,
):
    @pl.when(pl.program_id(0) == 0)
    def _():
        state[...] = jnp.zeros_like(state)

    cosine, sine = cos_ref[...], sin_ref[...]
    for h in range(heads):
        state_low = low_ref[0, h]
        inner_decay, place_decay, key_decay = inner_ref[h], place_ref[h], key_ref[h]
        query, key, value, gate, weights, grouped, factor = head_forward(
            h, heads, pre_ref, cosine, sine, inner_decay, place_decay, state_low
        )
        q_at, k_at = h * KHEAD, (heads + h) * KHEAD
        v_at, g_at = 2 * heads * KHEAD + h * VHEAD, 2 * heads * KHEAD + (heads + h) * VHEAD
        d_gated = grad_ref[:, h * VHEAD : (h + 1) * VHEAD]
        sigma = jax.nn.sigmoid(gate)
        swish = gate * sigma
        out_ref[:, g_at : g_at + VHEAD] = (
            d_gated * grouped * (sigma + swish * (1.0 - sigma))
        ).astype(BF16)
        d_retained = layer_back(d_gated * swish, grouped, factor)
        d_inner = d_retained.astype(BF16)
        d_carried = (d_retained * place_decay).astype(BF16)
        d_scores = (contract_cols(d_inner, value) * inner_decay).astype(BF16)
        after = state[h]
        local_grad = after.astype(BF16)
        key_scaled = (key.astype(F32) * key_decay).astype(BF16)
        d_query = dot(d_scores, key) + contract_cols(d_carried, state_low)
        d_key = contract_rows(d_scores, query) + key_decay * contract_cols(value, local_grad)
        d_value = contract_rows(weights, d_inner) + dot(key_scaled, local_grad)
        out_ref[:, q_at : q_at + KHEAD] = unrotate(d_query, cosine, sine).astype(BF16)
        out_ref[:, k_at : k_at + KHEAD] = unrotate(d_key, cosine, sine).astype(BF16)
        out_ref[:, v_at : v_at + VHEAD] = d_value.astype(BF16)
        state[h] = after * block_ref[h] + contract_rows(query, d_carried)


def decays(heads, first):
    logs = lax.dynamic_slice(decay_logs(HEADS), (first,), (heads,))
    places = jnp.arange(SPAN, dtype=F32)
    spacing = places[:, None] - places[None, :]
    inner = jnp.where(
        spacing[None] >= 0, jnp.exp(jnp.maximum(spacing, 0.0)[None] * logs[:, None, None]), 0.0
    )
    place = jnp.exp(places[None, :] * logs[:, None])[:, :, None]
    key = jnp.exp((SPAN - places)[None, :] * logs[:, None])[:, :, None]
    return inner, place, key, jnp.exp(SPAN * logs)


def retention_call(heads, blocks, order, pre, tables, decay, extra):
    backward = bool(extra)
    wide, narrow = pre.shape[1], heads * VHEAD
    at = (lambda t: blocks - 1 - t) if backward else (lambda t: t)
    row = lambda t, order, *_: (order[at(t)], 0)
    place = lambda t, *_: (at(t), 0)
    whole = lambda t, *_: (0, 0, 0)
    low_spec = pl.BlockSpec((1, heads, KHEAD, VHEAD), lambda t, *_: (at(t), 0, 0, 0))
    in_specs = [
        pl.BlockSpec((SPAN, wide), row),
        pl.BlockSpec((SPAN, KHEAD // 2), place),
        pl.BlockSpec((SPAN, KHEAD // 2), place),
        pl.BlockSpec((heads, SPAN, SPAN), whole),
        pl.BlockSpec((heads, SPAN, 1), whole),
        pl.BlockSpec((heads, SPAN, 1), whole),
    ]
    inner, place_decay, key_decay, block_decay = decay
    if backward:
        in_specs += [low_spec, pl.BlockSpec((SPAN, narrow), row)]
        out_specs = pl.BlockSpec((SPAN, wide), row)
        out_shape = jax.ShapeDtypeStruct(pre.shape, BF16)
        body = retention_backward_kernel
    else:
        out_specs = (pl.BlockSpec((SPAN, narrow), row), low_spec)
        out_shape = (
            jax.ShapeDtypeStruct((pre.shape[0], narrow), BF16),
            jax.ShapeDtypeStruct((blocks, heads, KHEAD, VHEAD), BF16),
        )
        body = retention_forward_kernel
    products = (15 if backward else 7) * SPAN * SPAN * SPAN * 2 * heads * blocks
    return pl.pallas_call(
        functools.partial(body, heads),
        grid_spec=pltpu.PrefetchScalarGridSpec(
            num_scalar_prefetch=2,
            grid=(blocks,),
            in_specs=in_specs,
            out_specs=out_specs,
            scratch_shapes=[pltpu.VMEM((heads, KHEAD, VHEAD), F32)],
        ),
        out_shape=out_shape,
        compiler_params=pltpu.CompilerParams(vmem_limit_bytes=48 * 1024 * 1024),
        cost_estimate=pl.CostEstimate(
            flops=products, bytes_accessed=pre.size * (6 if backward else 5), transcendentals=0
        ),
        name="retention_backward" if backward else "retention_forward",
    )(order, block_decay, pre, *tables, inner, place_decay, key_decay, *extra)


def on_device(
    tokens,
    cotangent,
    domain,
    query_weight,
    key_weight,
    value_weight,
    gate_weight,
    output_weight,
    retention_gain,
    retention_bias,
    feedfwd_gain,
    feedfwd_bias,
    up_weight,
    down_weight,
):
    dp, mp = lax.axis_size("dp"), lax.axis_size("mp")
    here = lax.axis_index("mp")
    masks = range(mp)
    rows = tokens.shape[0]
    total = rows * mp
    blocks = total // SPAN
    heads = HEADS // mp
    part = query_weight.shape[0]
    own = part * mp

    def swap(x, mask):
        if mask == 0:
            return x
        return lax.ppermute(x, "mp", [(s, s ^ mask) for s in range(mp)])

    def spread(x):
        return [swap(x, m) for m in masks]

    def collect(pieces):
        received = [swap(pieces[m].astype(BF16), m).astype(F32) for m in masks[1:]]
        return functools.reduce(jnp.add, received, pieces[0].astype(F32))

    def by_index(pieces):
        stacked = jnp.stack(pieces)
        return [
            lax.dynamic_index_in_dim(stacked, here ^ m, 0, keepdims=False) for m in masks
        ]

    thin = jnp.stack(
        [retention_gain, retention_bias, feedfwd_gain, feedfwd_bias]
        + [jnp.broadcast_to(domain.astype(BF16), (part,))],
        axis=1,
    )
    thin = jnp.pad(thin, ((0, 0), (0, 128 - thin.shape[1])))

    def columns(weight, target):
        width = weight.shape[1] // mp
        return lax.dynamic_slice(weight, (0, target * width), (part, width))

    pieces = []
    for m in masks:
        target = here ^ m
        pieces.append(
            jnp.concatenate(
                [columns(w, target) for w in (query_weight, key_weight, value_weight, gate_weight)]
                + [thin],
                axis=1,
            )
        )
    pieces = by_index([swap(pieces[m], m) for m in masks])
    packed = jnp.concatenate(pieces, axis=0)
    wide = packed.shape[1] - 128
    thin_all = lax.all_gather(packed[:, wide : wide + 8], "dp", axis=0, tiled=True)
    gain_one, bias_one, gain_two, bias_two = (thin_all[:, n].astype(F32)[None] for n in range(4))
    w_in = lax.all_gather(packed[:, :wide], "dp", axis=0, tiled=True)

    shuffle = [(b, (b % dp) * mp + b // dp) for b in range(dp * mp)]
    w_out = lax.all_gather(
        lax.ppermute(output_weight, ("dp", "mp"), shuffle), "dp", axis=0, tiled=True
    )
    w_up = lax.all_gather(up_weight, "dp", axis=0, tiled=True)
    w_down = lax.all_gather(down_weight.T, "dp", axis=0, tiled=True)

    source_rows = jnp.concatenate(spread(tokens), axis=0)
    cotan_rows = jnp.concatenate(spread(cotangent), axis=0)

    domains = thin_all[::own, 4]
    own_count = jnp.sum((domains == domain[0].astype(BF16)).astype(F32)) * (rows * mp)
    row_scale = F32(rows * dp * mp) / (DOMAINS * own_count)

    tables = rotation_tables(total, KHEAD)
    decay = decays(heads, here * heads)
    block_order = (
        (jnp.arange(mp, dtype=jnp.int32) ^ here)[:, None] * (rows // SPAN)
        + jnp.arange(rows // SPAN, dtype=jnp.int32)[None]
    ).reshape(-1)

    normal_rows, _ = layer_stats(source_rows.astype(F32))
    normed_one = (normal_rows * gain_one + bias_one).astype(BF16)
    pre = dot(normed_one, w_in)
    gated, state_low = retention_call(heads, blocks, block_order, pre, tables, decay, ())

    def by_piece(x):
        return [x[m * rows : (m + 1) * rows] for m in masks]

    source = tokens.astype(F32)
    middle = source + collect([dot(piece, w_out) for piece in by_piece(gated)])
    normal_two, factor_two = layer_stats(middle)
    normed_two = (normal_two * gain_two + bias_two).astype(BF16)
    normed_rows = jnp.concatenate(spread(normed_two), axis=0)
    hidden_pre = dot(normed_rows, w_up)
    hidden = jax.nn.gelu(hidden_pre).astype(BF16)
    feed_sum = collect([contract_cols(piece, w_down) for piece in by_piece(hidden)])
    outputs = (middle + feed_sum).astype(BF16)

    grad_rows = (cotan_rows.astype(F32) * row_scale).astype(BF16)
    d_hidden = dot(grad_rows, w_down)
    _, gelu_pull = jax.vjp(jax.nn.gelu, hidden_pre)
    d_pre = gelu_pull(d_hidden)[0].astype(BF16)
    d_normed_two = collect([contract_cols(piece, w_up) for piece in by_piece(d_pre)])
    down_part = contract_rows(grad_rows, hidden).astype(BF16)
    up_part = contract_rows(normed_rows, d_pre).astype(BF16)

    cotan = cotangent.astype(F32) * row_scale
    d_middle = cotan + layer_back(d_normed_two * gain_two, normal_two, factor_two)
    branch_rows = jnp.concatenate(spread(d_middle.astype(BF16)), axis=0)
    d_gated = contract_cols(branch_rows, w_out)
    output_part = contract_rows(gated, branch_rows).astype(BF16)
    d_in = retention_call(
        heads, blocks, block_order, pre, tables, decay, (state_low, d_gated)
    )
    in_part = contract_rows(normed_one, d_in).astype(BF16)
    d_normed_one = collect([contract_cols(piece, w_in) for piece in by_piece(d_in)])
    normal_one, factor_one = layer_stats(source)
    d_tokens = d_middle + layer_back(d_normed_one * gain_one, normal_one, factor_one)

    scatter = functools.partial(
        lax.psum_scatter, axis_name="dp", scatter_dimension=0, tiled=True
    )
    down_grad = scatter(down_part).astype(F32).T
    up_grad = scatter(up_part).astype(F32)
    unshuffle = [(target, at) for at, target in shuffle]
    output_grad = lax.ppermute(scatter(output_part), ("dp", "mp"), unshuffle).astype(F32)
    in_grad = scatter(in_part)
    pieces = by_index([in_grad[m * part : (m + 1) * part] for m in masks])
    pieces = by_index([swap(pieces[m], m) for m in masks])
    grads, at = [], 0
    for weight in (query_weight, key_weight, value_weight, gate_weight):
        width = weight.shape[1] // mp
        grads.append(
            jnp.concatenate([p[:, at : at + width] for p in pieces], axis=1).astype(F32)
        )
        at += width

    thin_grads = jnp.stack(
        [
            jnp.sum(d_normed_one * normal_one, axis=0),
            jnp.sum(d_normed_one, axis=0),
            jnp.sum(d_normed_two * normal_two, axis=0),
            jnp.sum(d_normed_two, axis=0),
        ],
        axis=0,
    )
    thin_grads = lax.psum_scatter(
        thin_grads, ("dp", "mp"), scatter_dimension=1, tiled=True
    )
    return (
        outputs,
        d_tokens.astype(BF16),
        *grads,
        output_grad,
        *(thin_grads[n] for n in range(4)),
        up_grad,
        down_grad,
    )


def solution(mesh):
    return jax.shard_map(
        on_device,
        mesh=mesh,
        in_specs=(
            P(("dp", "mp"), None),
            P(("dp", "mp"), None),
            P("dp"),
            P(("dp", "mp"), None),
            P(("dp", "mp"), None),
            P(("dp", "mp"), None),
            P(("dp", "mp"), None),
            P(("dp", "mp"), None),
            P(("dp", "mp")),
            P(("dp", "mp")),
            P(("dp", "mp")),
            P(("dp", "mp")),
            P("dp", "mp"),
            P("mp", "dp"),
        ),
        out_specs=(
            P(("dp", "mp"), None),
            P(("dp", "mp"), None),
            P(("dp", "mp"), None),
            P(("dp", "mp"), None),
            P(("dp", "mp"), None),
            P(("dp", "mp"), None),
            P(("dp", "mp"), None),
            P(("dp", "mp")),
            P(("dp", "mp")),
            P(("dp", "mp")),
            P(("dp", "mp")),
            P("dp", "mp"),
            P("mp", "dp"),
        ),
        check_vma=False,
    )
```

```python
import functools

import jax
import jax.numpy as jnp
from jax import lax
from jax.experimental import pallas as pl
from jax.experimental.pallas import tpu as pltpu
from jax.sharding import PartitionSpec as P

D = 2048
DV = 4096
HEADS = 8
KHEAD = 256
VHEAD = 512
SPAN = 256
DOMAINS = 4


EPSILON = 1e-05
F32 = jnp.float32
BF16 = jnp.bfloat16


def layer_stats(values):
    center = values - jnp.mean(values, axis=-1, keepdims=True)
    factor = lax.rsqrt(jnp.mean(center * center, axis=-1, keepdims=True) + EPSILON)
    return (center * factor, factor)


def layer_back(grad, normal, factor):
    return factor * (
        grad
        - jnp.mean(grad, axis=-1, keepdims=True)
        - normal * jnp.mean(grad * normal, axis=-1, keepdims=True)
    )


def decay_logs(heads):
    return jnp.log1p(-jnp.exp2(-5.0 - jnp.arange(heads, dtype=jnp.float32)))


def rotation_tables(count, width):
    freq = 10000.0 ** (-2.0 * jnp.arange(width // 2, dtype=jnp.float32) / width)
    places = jnp.arange(count, dtype=jnp.int32).astype(jnp.float32)
    angle = places[:, None] * freq[None, :]
    return (jnp.cos(angle), jnp.sin(angle))


def dot(left, right):
    return jnp.dot(left, right, preferred_element_type=F32)


def contract_rows(left, right):
    return lax.dot_general(
        left, right, (((0,), (0,)), ((), ())), preferred_element_type=F32
    )


def contract_cols(left, right):
    return lax.dot_general(
        left, right, (((1,), (1,)), ((), ())), preferred_element_type=F32
    )


def rotate(values, cosine, sine):
    half = values.shape[-1] // 2
    first, second = values[:, :half], values[:, half:]
    return jnp.concatenate(
        [first * cosine - second * sine, first * sine + second * cosine], axis=-1
    )


def unrotate(values, cosine, sine):
    half = values.shape[-1] // 2
    first, second = values[:, :half], values[:, half:]
    return jnp.concatenate(
        [first * cosine + second * sine, second * cosine - first * sine], axis=-1
    )


def head_forward(h, heads, pre_ref, cosine, sine, inner_decay, place_decay, state_low):
    q_at, k_at = h * KHEAD, (heads + h) * KHEAD
    v_at, g_at = 2 * heads * KHEAD + h * VHEAD, 2 * heads * KHEAD + (heads + h) * VHEAD
    query = rotate(pre_ref[:, q_at : q_at + KHEAD], cosine, sine).astype(BF16)
    key = rotate(pre_ref[:, k_at : k_at + KHEAD], cosine, sine).astype(BF16)
    value = pre_ref[:, v_at : v_at + VHEAD].astype(BF16)
    gate = pre_ref[:, g_at : g_at + VHEAD]
    weights = (contract_cols(query, key) * inner_decay).astype(BF16)
    retained = dot(weights, value) + dot(query, state_low) * place_decay
    grouped, factor = layer_stats(retained)
    return query, key, value, gate, weights, grouped, factor


def retention_forward_kernel(
    heads, order_ref, block_ref, pre_ref, cos_ref, sin_ref, inner_ref, place_ref, key_ref,
    gated_ref, low_ref, state,
):
    @pl.when(pl.program_id(0) == 0)
    def _():
        state[...] = jnp.zeros_like(state)

    cosine, sine = cos_ref[...], sin_ref[...]
    for h in range(heads):
        before = state[h]
        state_low = before.astype(BF16)
        low_ref[0, h] = state_low
        query, key, value, gate, weights, grouped, factor = head_forward(
            h, heads, pre_ref, cosine, sine, inner_ref[h], place_ref[h], state_low
        )
        gated = gate * jax.nn.sigmoid(gate) * grouped
        gated_ref[:, h * VHEAD : (h + 1) * VHEAD] = gated.astype(BF16)
        key_scaled = (key.astype(F32) * key_ref[h]).astype(BF16)
        state[h] = before * block_ref[h] + contract_rows(key_scaled, value)


def retention_backward_kernel(
    heads, order_ref, block_ref, pre_ref, cos_ref, sin_ref, inner_ref, place_ref, key_ref,
    low_ref, grad_ref, out_ref, state,
):
    @pl.when(pl.program_id(0) == 0)
    def _():
        state[...] = jnp.zeros_like(state)

    cosine, sine = cos_ref[...], sin_ref[...]
    for h in range(heads):
        state_low = low_ref[0, h]
        inner_decay, place_decay, key_decay = inner_ref[h], place_ref[h], key_ref[h]
        query, key, value, gate, weights, grouped, factor = head_forward(
            h, heads, pre_ref, cosine, sine, inner_decay, place_decay, state_low
        )
        q_at, k_at = h * KHEAD, (heads + h) * KHEAD
        v_at, g_at = 2 * heads * KHEAD + h * VHEAD, 2 * heads * KHEAD + (heads + h) * VHEAD
        d_gated = grad_ref[:, h * VHEAD : (h + 1) * VHEAD]
        sigma = jax.nn.sigmoid(gate)
        swish = gate * sigma
        out_ref[:, g_at : g_at + VHEAD] = (
            d_gated * grouped * (sigma + swish * (1.0 - sigma))
        ).astype(BF16)
        d_retained = layer_back(d_gated * swish, grouped, factor)
        d_inner = d_retained.astype(BF16)
        d_carried = (d_retained * place_decay).astype(BF16)
        d_scores = (contract_cols(d_inner, value) * inner_decay).astype(BF16)
        after = state[h]
        local_grad = after.astype(BF16)
        key_scaled = (key.astype(F32) * key_decay).astype(BF16)
        d_query = dot(d_scores, key) + contract_cols(d_carried, state_low)
        d_key = contract_rows(d_scores, query) + key_decay * contract_cols(value, local_grad)
        d_value = contract_rows(weights, d_inner) + dot(key_scaled, local_grad)
        out_ref[:, q_at : q_at + KHEAD] = unrotate(d_query, cosine, sine).astype(BF16)
        out_ref[:, k_at : k_at + KHEAD] = unrotate(d_key, cosine, sine).astype(BF16)
        out_ref[:, v_at : v_at + VHEAD] = d_value.astype(BF16)
        state[h] = after * block_ref[h] + contract_rows(query, d_carried)


def decays(heads, first):
    logs = lax.dynamic_slice(decay_logs(HEADS), (first,), (heads,))
    places = jnp.arange(SPAN, dtype=F32)
    spacing = places[:, None] - places[None, :]
    inner = jnp.where(
        spacing[None] >= 0, jnp.exp(jnp.maximum(spacing, 0.0)[None] * logs[:, None, None]), 0.0
    )
    place = jnp.exp(places[None, :] * logs[:, None])[:, :, None]
    key = jnp.exp((SPAN - places)[None, :] * logs[:, None])[:, :, None]
    return inner, place, key, jnp.exp(SPAN * logs)


def retention_call(heads, blocks, order, pre, tables, decay, extra):
    backward = bool(extra)
    wide, narrow = pre.shape[1], heads * VHEAD
    at = (lambda t: blocks - 1 - t) if backward else (lambda t: t)
    row = lambda t, order, *_: (order[at(t)], 0)
    place = lambda t, *_: (at(t), 0)
    whole = lambda t, *_: (0, 0, 0)
    low_spec = pl.BlockSpec((1, heads, KHEAD, VHEAD), lambda t, *_: (at(t), 0, 0, 0))
    in_specs = [
        pl.BlockSpec((SPAN, wide), row),
        pl.BlockSpec((SPAN, KHEAD // 2), place),
        pl.BlockSpec((SPAN, KHEAD // 2), place),
        pl.BlockSpec((heads, SPAN, SPAN), whole),
        pl.BlockSpec((heads, SPAN, 1), whole),
        pl.BlockSpec((heads, SPAN, 1), whole),
    ]
    inner, place_decay, key_decay, block_decay = decay
    if backward:
        in_specs += [low_spec, pl.BlockSpec((SPAN, narrow), row)]
        out_specs = pl.BlockSpec((SPAN, wide), row)
        out_shape = jax.ShapeDtypeStruct(pre.shape, BF16)
        body = retention_backward_kernel
    else:
        out_specs = (pl.BlockSpec((SPAN, narrow), row), low_spec)
        out_shape = (
            jax.ShapeDtypeStruct((pre.shape[0], narrow), BF16),
            jax.ShapeDtypeStruct((blocks, heads, KHEAD, VHEAD), BF16),
        )
        body = retention_forward_kernel
    products = (15 if backward else 7) * SPAN * SPAN * SPAN * 2 * heads * blocks
    return pl.pallas_call(
        functools.partial(body, heads),
        grid_spec=pltpu.PrefetchScalarGridSpec(
            num_scalar_prefetch=2,
            grid=(blocks,),
            in_specs=in_specs,
            out_specs=out_specs,
            scratch_shapes=[pltpu.VMEM((heads, KHEAD, VHEAD), F32)],
        ),
        out_shape=out_shape,
        compiler_params=pltpu.CompilerParams(vmem_limit_bytes=48 * 1024 * 1024),
        cost_estimate=pl.CostEstimate(
            flops=products, bytes_accessed=pre.size * (6 if backward else 5), transcendentals=0
        ),
        name="retention_backward" if backward else "retention_forward",
    )(order, block_decay, pre, *tables, inner, place_decay, key_decay, *extra)


def product_kernel(contract, a_ref, b_ref, *out_refs):
    result = lax.dot_general(
        a_ref[...], b_ref[...], (contract, ((), ())), preferred_element_type=F32
    )
    step = result.shape[0] // len(out_refs)
    for n, out_ref in enumerate(out_refs):
        out_ref[...] = result[n * step : (n + 1) * step].astype(BF16)


def row_product(a, b, transposed, parts, column=0):
    rows, depth = a.shape
    width = b.shape[0] if transposed else b.shape[1]
    tile = min(512, width)
    if transposed:
        b_spec = pl.BlockSpec((tile, depth), lambda n: (n, column))
    else:
        b_spec = pl.BlockSpec((depth, tile), lambda n: (0, n))
    return pl.pallas_call(
        functools.partial(product_kernel, ((1,), (1 if transposed else 0,))),
        grid=(width // tile,),
        in_specs=[pl.BlockSpec((rows, depth), lambda n: (0, 0)), b_spec],
        out_specs=[pl.BlockSpec((rows // parts, tile), lambda n: (0, n))] * parts,
        out_shape=[jax.ShapeDtypeStruct((rows // parts, width), BF16)] * parts,
        compiler_params=pltpu.CompilerParams(vmem_limit_bytes=48 * 1024 * 1024),
        cost_estimate=pl.CostEstimate(
            flops=2 * rows * depth * width,
            bytes_accessed=2 * (rows * depth + depth * width + rows * width),
            transcendentals=0,
        ),
        name="row_product",
    )(a, b)


def feed_kernel(
    steps, normed_ref, grad_ref, up_ref, down_ref, up_row_ref, hidden_ref, pre_ref, *out_refs
):
    step = pl.program_id(0)

    @pl.when(step < steps)
    def _():
        u = dot(normed_ref[...], up_ref[...])
        d_hidden = dot(grad_ref[...], down_ref[...])
        scale = 0.7978845608028654
        square = u * u
        t = jnp.tanh(scale * u * (1.0 + 0.044715 * square))
        half = 0.5 * (1.0 + t)
        hidden_ref[...] = (u * half).astype(BF16)
        slope = half + 0.5 * scale * u * (1.0 - t * t) * (1.0 + 3 * 0.044715 * square)
        tile = u.shape[1]
        pre_ref[:, pl.ds(pl.multiple_of(step * tile, tile), tile)] = (d_hidden * slope).astype(BF16)

    @pl.when(step >= steps)
    def _():
        result = contract_cols(pre_ref[...], up_row_ref[...])
        count = result.shape[0] // len(out_refs)
        for n, out_ref in enumerate(out_refs):
            out_ref[...] = result[n * count : (n + 1) * count].astype(BF16)


def feed_call(normed, grad, both, parts):
    rows, depth = normed.shape
    width = both.shape[1] // 2
    tile, out_tile = min(256, width), min(512, depth)
    steps, out_steps = width // tile, depth // out_tile
    first = lambda n: jnp.minimum(n, steps - 1)
    second = lambda n: jnp.maximum(n - steps, 0)
    whole = pl.BlockSpec((rows, depth), lambda n: (0, 0))
    return pl.pallas_call(
        functools.partial(feed_kernel, steps),
        grid=(steps + out_steps,),
        in_specs=[
            whole,
            whole,
            pl.BlockSpec((depth, tile), lambda n: (0, first(n))),
            pl.BlockSpec((depth, tile), lambda n: (0, steps + first(n))),
            pl.BlockSpec((out_tile, width), lambda n: (second(n), 0)),
        ],
        out_specs=[
            pl.BlockSpec((rows, tile), lambda n: (0, first(n))),
            pl.BlockSpec((rows, width), lambda n: (0, 0)),
        ]
        + [pl.BlockSpec((rows // parts, out_tile), lambda n: (0, second(n)))] * parts,
        out_shape=[jax.ShapeDtypeStruct((rows, width), BF16)] * 2
        + [jax.ShapeDtypeStruct((rows // parts, depth), BF16)] * parts,
        compiler_params=pltpu.CompilerParams(vmem_limit_bytes=56 * 1024 * 1024),
        cost_estimate=pl.CostEstimate(
            flops=6 * rows * depth * width,
            bytes_accessed=4 * (rows * depth + depth * width + rows * width),
            transcendentals=rows * width,
        ),
        name="feed_forward",
    )(normed, grad, both, both, both)


def feed_grads_kernel(normed_ref, grad_ref, hidden_ref, pre_ref, out_ref):
    width = hidden_ref.shape[1]
    out_ref[:, :width] = contract_rows(normed_ref[...], pre_ref[...]).astype(BF16)
    out_ref[:, width:] = contract_rows(grad_ref[...], hidden_ref[...]).astype(BF16)


def feed_grads(normed, grad, hidden, d_pre):
    rows, depth = normed.shape
    width = hidden.shape[1]
    tile = min(512, depth)
    slab = pl.BlockSpec((rows, tile), lambda n: (0, n))
    whole = pl.BlockSpec((rows, width), lambda n: (0, 0))
    return pl.pallas_call(
        feed_grads_kernel,
        grid=(depth // tile,),
        in_specs=[slab, slab, whole, whole],
        out_specs=pl.BlockSpec((tile, 2 * width), lambda n: (n, 0)),
        out_shape=jax.ShapeDtypeStruct((depth, 2 * width), BF16),
        compiler_params=pltpu.CompilerParams(vmem_limit_bytes=48 * 1024 * 1024),
        cost_estimate=pl.CostEstimate(
            flops=4 * rows * depth * width,
            bytes_accessed=4 * (rows * depth + depth * width + rows * width),
            transcendentals=0,
        ),
        name="feed_grads",
    )(normed, grad, hidden, d_pre)


def on_device(
    tokens,
    cotangent,
    domain,
    query_weight,
    key_weight,
    value_weight,
    gate_weight,
    output_weight,
    retention_gain,
    retention_bias,
    feedfwd_gain,
    feedfwd_bias,
    up_weight,
    down_weight,
):
    dp, mp = lax.axis_size("dp"), lax.axis_size("mp")
    here = lax.axis_index("mp")
    masks = range(mp)
    rows = tokens.shape[0]
    total = rows * mp
    blocks = total // SPAN
    heads = HEADS // mp
    part = query_weight.shape[0]
    own = part * mp
    square = mp == 4
    parts = 2 * mp if square else mp
    together = lax.optimization_barrier

    def swap(x, mask):
        if mask == 0:
            return x
        return lax.ppermute(x, "mp", [(s, s ^ mask) for s in range(mp)])

    def spread(x):
        if not square:
            return jnp.concatenate([swap(x, m) for m in masks], axis=0)
        half = x.shape[0] // 2
        a, b = x[:half], x[half:]
        a1, b2 = swap(a, 1), swap(b, 2)
        a2, b1 = swap(a, 2), swap(b, 1)
        a3, b3 = swap(a1, 2), swap(b2, 1)
        return jnp.concatenate([a, b, a1, b1, a2, b2, a3, b3], axis=0)

    def collect(pieces, meanwhile=()):
        if not square:
            received = [swap(pieces[m], m) for m in masks[1:]]
            *received, meanwhile = together((*received, meanwhile))
            received = [r.astype(F32) for r in received]
            return functools.reduce(jnp.add, received, pieces[0].astype(F32)), meanwhile
        a0, b0, a1, b1, a2, b2, a3, b3 = pieces
        a3, b3 = swap(a3, 1), swap(b3, 2)
        a1, b2 = swap(a1, 1), swap(b2, 2)
        a3, b3, meanwhile = together((a3, b3, meanwhile))
        a2 = swap((a2.astype(F32) + a3.astype(F32)).astype(BF16), 2)
        b1 = swap((b1.astype(F32) + b3.astype(F32)).astype(BF16), 1)
        total = jnp.concatenate(
            [
                a0.astype(F32) + a1.astype(F32) + a2.astype(F32),
                b0.astype(F32) + b1.astype(F32) + b2.astype(F32),
            ],
            axis=0,
        )
        return total, meanwhile

    def shuffle(x, back=False):
        flat = [(b, (b % dp) * mp + b // dp) for b in range(dp * mp)]
        if not (dp == 8 and square):
            pairs = [(d, s) for s, d in flat] if back else flat
            return lambda late: lax.ppermute(x, ("dp", "mp"), pairs)
        first, second = ([], []), ([], [])
        for z in range(4):
            for c in range(2):
                for j in range(4):
                    plane = 2 * c + j // 2
                    start, middle = (2 * z + c) * 4 + j, (2 * plane + z % 2) * 4 + j
                    first[z // 2].append((start, middle))
                    second[z // 2].append((middle, (2 * plane + j % 2) * 4 + z))
        flipped = lambda pairs: [(d, s) for s, d in pairs]
        move = lambda v, pairs: lax.ppermute(v, ("dp", "mp"), pairs)
        if not back:
            low, high = (move(x, pairs) for pairs in first)

            def finish(late):
                a, b, late = together((low, high, late))
                return jnp.where(here < 2, move(a, second[0]), move(b, second[1]))

            return finish
        low, high = (move(x, flipped(pairs)) for pairs in second)
        upper = lax.axis_index("dp") >= 4

        def finish_back(late):
            a, b, late = together((low, high, late))
            return jnp.where(upper, move(b, flipped(first[1])), move(a, flipped(first[0])))

        return finish_back

    def scatter_small(x):
        cur = x.reshape(dp, mp, x.shape[-1])
        for dim, name in ((1, "mp"), (0, "dp")):
            index = lax.axis_index(name)
            while cur.shape[dim] > 1:
                count = cur.shape[dim] // 2
                bit = (index // count) % 2
                mine = lax.dynamic_slice_in_dim(cur, bit * count, count, dim)
                other = lax.dynamic_slice_in_dim(cur, (1 - bit) * count, count, dim)
                pairs = [(s, s ^ count) for s in range(lax.axis_size(name))]
                cur = mine + lax.ppermute(other, name, pairs)
        return cur.reshape(-1)

    def by_index(pieces):
        stacked = jnp.stack(pieces)
        return [
            lax.dynamic_index_in_dim(stacked, here ^ m, 0, keepdims=False) for m in masks
        ]

    thin = jnp.concatenate(
        [retention_gain, retention_bias, feedfwd_gain, feedfwd_bias]
        + [jnp.broadcast_to(domain.astype(BF16), (part,))]
    )
    thin = lax.all_gather(thin[None], "dp", axis=0, tiled=True)

    def columns(weight, target):
        width = weight.shape[1] // mp
        return lax.dynamic_slice(weight, (0, target * width), (part, width))

    pieces = []
    for m in masks:
        target = here ^ m
        pieces.append(
            jnp.concatenate(
                [columns(w, target) for w in (query_weight, key_weight, value_weight, gate_weight)],
                axis=1,
            )
        )
    *pieces, thin = together((*(swap(pieces[m], m) for m in masks), thin))
    packed = jnp.concatenate(by_index(pieces), axis=0)
    w_in = lax.all_gather(packed, "dp", axis=0, tiled=True)

    finish = shuffle(output_weight)
    tokens_late, cotangent_late, packed = together((tokens, cotangent, packed))
    thin = jnp.stack(by_index([swap(thin, m) for m in masks]))
    source_rows = spread(tokens_late)
    cotan_rows = spread(cotangent_late)
    shuffled = finish(packed)
    thin = thin.reshape(mp, dp, 5, part).transpose(2, 1, 0, 3).reshape(5, dp * own)
    gain_one, bias_one, gain_two, bias_two = (thin[n].astype(F32)[None] for n in range(4))

    domains = thin[4, ::own]
    own_count = jnp.sum((domains == domain[0].astype(BF16)).astype(F32)) * (rows * mp)
    row_scale = F32(rows * dp * mp) / (DOMAINS * own_count)

    tables = rotation_tables(total, KHEAD)
    decay = decays(heads, here * heads)
    block_order = (
        (jnp.arange(mp, dtype=jnp.int32) ^ here)[:, None] * (rows // SPAN)
        + jnp.arange(rows // SPAN, dtype=jnp.int32)[None]
    ).reshape(-1)

    normal_rows, _ = layer_stats(source_rows.astype(F32))
    normed_one = (normal_rows * gain_one + bias_one).astype(BF16)
    grad_rows = (cotan_rows.astype(F32) * row_scale).astype(BF16)
    normed_one, grad_rows, tables, decay = together((normed_one, grad_rows, tables, decay))
    w_out = lax.all_gather(shuffled, "dp", axis=0, tiled=True)
    w_feed = lax.all_gather(
        jnp.concatenate([up_weight, down_weight.T], axis=1), "dp", axis=0, tiled=True
    )

    pre = dot(normed_one, w_in)
    gated, state_low = retention_call(heads, blocks, block_order, pre, tables, decay, ())

    source = tokens.astype(F32)
    middle = source + collect(row_product(gated, w_out, False, parts))[0]
    normal_two, factor_two = layer_stats(middle)
    normed_two = (normal_two * gain_two + bias_two).astype(BF16)
    normed_rows = spread(normed_two)
    hidden, d_pre, *pieces = feed_call(normed_rows, grad_rows, w_feed, parts)
    *pieces, hidden, d_pre = together((*pieces, hidden, d_pre))
    feed_part = feed_grads(normed_rows, grad_rows, hidden, d_pre)
    d_normed_two, feed_part = collect(pieces, feed_part)
    scatter = functools.partial(
        lax.psum_scatter, axis_name="dp", scatter_dimension=0, tiled=True
    )
    feed_grad = scatter(feed_part)

    cotan = cotangent.astype(F32) * row_scale
    d_middle = cotan + layer_back(d_normed_two * gain_two, normal_two, factor_two)
    branch_rows = spread(d_middle.astype(BF16))
    d_gated = contract_cols(branch_rows, w_out)
    d_in = retention_call(
        heads, blocks, block_order, pre, tables, decay, (state_low, d_gated)
    )
    d_in, branch_rows, feed_grad = together((d_in, branch_rows, feed_grad))
    output_part = contract_rows(gated, branch_rows).astype(BF16)
    d_in, output_part = together((d_in, output_part))
    in_part = contract_rows(normed_one, d_in).astype(BF16)
    d_in, in_part, hidden = together((d_in, in_part, hidden))
    d_normed_one, _ = collect(row_product(d_in, w_in, True, parts))
    normal_one, factor_one = layer_stats(source)
    d_tokens = d_middle + layer_back(d_normed_one * gain_one, normal_one, factor_one)

    feed_sum, _ = collect(row_product(hidden, w_feed, True, parts, 1))
    outputs = (middle + feed_sum).astype(BF16)

    width = up_weight.shape[1]
    up_grad = feed_grad[:, :width].astype(F32)
    down_grad = feed_grad[:, width:].astype(F32).T
    finish = shuffle(scatter(output_part), True)
    in_grad = scatter(in_part)
    output_grad = finish(in_grad).astype(F32)
    pieces = by_index([in_grad[m * part : (m + 1) * part] for m in masks])
    pieces = by_index([swap(pieces[m], m) for m in masks])
    grads, at = [], 0
    for weight in (query_weight, key_weight, value_weight, gate_weight):
        width = weight.shape[1] // mp
        grads.append(
            jnp.concatenate([p[:, at : at + width] for p in pieces], axis=1).astype(F32)
        )
        at += width

    thin_grads = jnp.stack(
        [
            jnp.sum(d_normed_one * normal_one, axis=0),
            jnp.sum(d_normed_one, axis=0),
            jnp.sum(d_normed_two * normal_two, axis=0),
            jnp.sum(d_normed_two, axis=0),
        ],
        axis=0,
    )
    thin_grads = thin_grads.reshape(4, dp * mp, part).transpose(1, 0, 2).reshape(dp * mp, 4 * part)
    thin_grads = scatter_small(thin_grads).reshape(4, part)
    return (
        outputs,
        d_tokens.astype(BF16),
        *grads,
        output_grad,
        *(thin_grads[n] for n in range(4)),
        up_grad,
        down_grad,
    )


def solution(mesh):
    return jax.shard_map(
        on_device,
        mesh=mesh,
        in_specs=(
            P(("dp", "mp"), None),
            P(("dp", "mp"), None),
            P("dp"),
            P(("dp", "mp"), None),
            P(("dp", "mp"), None),
            P(("dp", "mp"), None),
            P(("dp", "mp"), None),
            P(("dp", "mp"), None),
            P(("dp", "mp")),
            P(("dp", "mp")),
            P(("dp", "mp")),
            P(("dp", "mp")),
            P("dp", "mp"),
            P("mp", "dp"),
        ),
        out_specs=(
            P(("dp", "mp"), None),
            P(("dp", "mp"), None),
            P(("dp", "mp"), None),
            P(("dp", "mp"), None),
            P(("dp", "mp"), None),
            P(("dp", "mp"), None),
            P(("dp", "mp"), None),
            P(("dp", "mp")),
            P(("dp", "mp")),
            P(("dp", "mp")),
            P(("dp", "mp")),
            P("dp", "mp"),
            P("mp", "dp"),
        ),
        check_vma=False,
    )
```

```python
import functools

import jax
import jax.numpy as jnp
from jax import lax
from jax.experimental import pallas as pl
from jax.experimental.pallas import tpu as pltpu
from jax.sharding import PartitionSpec as P

D = 2048
DV = 4096
HEADS = 8
KHEAD = 256
VHEAD = 512
SPAN = 256
DOMAINS = 4


EPSILON = 1e-05
F32 = jnp.float32
BF16 = jnp.bfloat16


def layer_stats(values):
    center = values - jnp.mean(values, axis=-1, keepdims=True)
    factor = lax.rsqrt(jnp.mean(center * center, axis=-1, keepdims=True) + EPSILON)
    return (center * factor, factor)


def layer_back(grad, normal, factor):
    return factor * (
        grad
        - jnp.mean(grad, axis=-1, keepdims=True)
        - normal * jnp.mean(grad * normal, axis=-1, keepdims=True)
    )


def decay_logs(heads):
    return jnp.log1p(-jnp.exp2(-5.0 - jnp.arange(heads, dtype=jnp.float32)))


def rotation_tables(count, width):
    freq = 10000.0 ** (-2.0 * jnp.arange(width // 2, dtype=jnp.float32) / width)
    places = jnp.arange(count, dtype=jnp.int32).astype(jnp.float32)
    angle = places[:, None] * freq[None, :]
    return (jnp.cos(angle), jnp.sin(angle))


def dot(left, right):
    return jnp.dot(left, right, preferred_element_type=F32)


def contract_rows(left, right):
    return lax.dot_general(
        left, right, (((0,), (0,)), ((), ())), preferred_element_type=F32
    )


def contract_cols(left, right):
    return lax.dot_general(
        left, right, (((1,), (1,)), ((), ())), preferred_element_type=F32
    )


def rotate(values, cosine, sine):
    half = values.shape[-1] // 2
    first, second = values[:, :half], values[:, half:]
    return jnp.concatenate(
        [first * cosine - second * sine, first * sine + second * cosine], axis=-1
    )


def unrotate(values, cosine, sine):
    half = values.shape[-1] // 2
    first, second = values[:, :half], values[:, half:]
    return jnp.concatenate(
        [first * cosine + second * sine, second * cosine - first * sine], axis=-1
    )


def head_forward(h, heads, pre_ref, cosine, sine, inner_decay, place_decay, state_low):
    q_at, k_at = h * KHEAD, (heads + h) * KHEAD
    v_at, g_at = 2 * heads * KHEAD + h * VHEAD, 2 * heads * KHEAD + (heads + h) * VHEAD
    query = rotate(pre_ref[:, q_at : q_at + KHEAD], cosine, sine).astype(BF16)
    key = rotate(pre_ref[:, k_at : k_at + KHEAD], cosine, sine).astype(BF16)
    value = pre_ref[:, v_at : v_at + VHEAD].astype(BF16)
    gate = pre_ref[:, g_at : g_at + VHEAD]
    weights = (contract_cols(query, key) * inner_decay).astype(BF16)
    retained = dot(weights, value) + dot(query, state_low) * place_decay
    grouped, factor = layer_stats(retained)
    return query, key, value, gate, weights, grouped, factor


def retention_forward_kernel(
    heads, order_ref, block_ref, pre_ref, cos_ref, sin_ref, inner_ref, place_ref, key_ref,
    gated_ref, low_ref, state,
):
    @pl.when(pl.program_id(0) == 0)
    def _():
        state[...] = jnp.zeros_like(state)

    cosine, sine = cos_ref[...], sin_ref[...]
    for h in range(heads):
        before = state[h]
        state_low = before.astype(BF16)
        low_ref[0, h] = state_low
        query, key, value, gate, weights, grouped, factor = head_forward(
            h, heads, pre_ref, cosine, sine, inner_ref[h], place_ref[h], state_low
        )
        gated = gate * jax.nn.sigmoid(gate) * grouped
        gated_ref[:, h * VHEAD : (h + 1) * VHEAD] = gated.astype(BF16)
        key_scaled = (key.astype(F32) * key_ref[h]).astype(BF16)
        state[h] = before * block_ref[h] + contract_rows(key_scaled, value)


def retention_backward_kernel(
    heads, order_ref, block_ref, pre_ref, cos_ref, sin_ref, inner_ref, place_ref, key_ref,
    low_ref, grad_ref, out_ref, state,
):
    @pl.when(pl.program_id(0) == 0)
    def _():
        state[...] = jnp.zeros_like(state)

    cosine, sine = cos_ref[...], sin_ref[...]
    for h in range(heads):
        state_low = low_ref[0, h]
        inner_decay, place_decay, key_decay = inner_ref[h], place_ref[h], key_ref[h]
        query, key, value, gate, weights, grouped, factor = head_forward(
            h, heads, pre_ref, cosine, sine, inner_decay, place_decay, state_low
        )
        q_at, k_at = h * KHEAD, (heads + h) * KHEAD
        v_at, g_at = 2 * heads * KHEAD + h * VHEAD, 2 * heads * KHEAD + (heads + h) * VHEAD
        d_gated = grad_ref[:, h * VHEAD : (h + 1) * VHEAD]
        sigma = jax.nn.sigmoid(gate)
        swish = gate * sigma
        out_ref[:, g_at : g_at + VHEAD] = (
            d_gated * grouped * (sigma + swish * (1.0 - sigma))
        ).astype(BF16)
        d_retained = layer_back(d_gated * swish, grouped, factor)
        d_inner = d_retained.astype(BF16)
        d_carried = (d_retained * place_decay).astype(BF16)
        d_scores = (contract_cols(d_inner, value) * inner_decay).astype(BF16)
        after = state[h]
        local_grad = after.astype(BF16)
        key_scaled = (key.astype(F32) * key_decay).astype(BF16)
        d_query = dot(d_scores, key) + contract_cols(d_carried, state_low)
        d_key = contract_rows(d_scores, query) + key_decay * contract_cols(value, local_grad)
        d_value = contract_rows(weights, d_inner) + dot(key_scaled, local_grad)
        out_ref[:, q_at : q_at + KHEAD] = unrotate(d_query, cosine, sine).astype(BF16)
        out_ref[:, k_at : k_at + KHEAD] = unrotate(d_key, cosine, sine).astype(BF16)
        out_ref[:, v_at : v_at + VHEAD] = d_value.astype(BF16)
        state[h] = after * block_ref[h] + contract_rows(query, d_carried)


def decays(heads, first):
    logs = lax.dynamic_slice(decay_logs(HEADS), (first,), (heads,))
    places = jnp.arange(SPAN, dtype=F32)
    spacing = places[:, None] - places[None, :]
    inner = jnp.where(
        spacing[None] >= 0, jnp.exp(jnp.maximum(spacing, 0.0)[None] * logs[:, None, None]), 0.0
    )
    place = jnp.exp(places[None, :] * logs[:, None])[:, :, None]
    key = jnp.exp((SPAN - places)[None, :] * logs[:, None])[:, :, None]
    return inner, place, key, jnp.exp(SPAN * logs)


def retention_call(heads, blocks, order, pre, tables, decay, extra):
    backward = bool(extra)
    wide, narrow = pre.shape[1], heads * VHEAD
    at = (lambda t: blocks - 1 - t) if backward else (lambda t: t)
    row = lambda t, order, *_: (order[at(t)], 0)
    place = lambda t, *_: (at(t), 0)
    whole = lambda t, *_: (0, 0, 0)
    low_spec = pl.BlockSpec((1, heads, KHEAD, VHEAD), lambda t, *_: (at(t), 0, 0, 0))
    in_specs = [
        pl.BlockSpec((SPAN, wide), row),
        pl.BlockSpec((SPAN, KHEAD // 2), place),
        pl.BlockSpec((SPAN, KHEAD // 2), place),
        pl.BlockSpec((heads, SPAN, SPAN), whole),
        pl.BlockSpec((heads, SPAN, 1), whole),
        pl.BlockSpec((heads, SPAN, 1), whole),
    ]
    inner, place_decay, key_decay, block_decay = decay
    if backward:
        in_specs += [low_spec, pl.BlockSpec((SPAN, narrow), row)]
        out_specs = pl.BlockSpec((SPAN, wide), row)
        out_shape = jax.ShapeDtypeStruct(pre.shape, BF16)
        body = retention_backward_kernel
    else:
        out_specs = (pl.BlockSpec((SPAN, narrow), row), low_spec)
        out_shape = (
            jax.ShapeDtypeStruct((pre.shape[0], narrow), BF16),
            jax.ShapeDtypeStruct((blocks, heads, KHEAD, VHEAD), BF16),
        )
        body = retention_forward_kernel
    products = (15 if backward else 7) * SPAN * SPAN * SPAN * 2 * heads * blocks
    return pl.pallas_call(
        functools.partial(body, heads),
        grid_spec=pltpu.PrefetchScalarGridSpec(
            num_scalar_prefetch=2,
            grid=(blocks,),
            in_specs=in_specs,
            out_specs=out_specs,
            scratch_shapes=[pltpu.VMEM((heads, KHEAD, VHEAD), F32)],
        ),
        out_shape=out_shape,
        compiler_params=pltpu.CompilerParams(vmem_limit_bytes=48 * 1024 * 1024),
        cost_estimate=pl.CostEstimate(
            flops=products, bytes_accessed=pre.size * (6 if backward else 5), transcendentals=0
        ),
        name="retention_backward" if backward else "retention_forward",
    )(order, block_decay, pre, *tables, inner, place_decay, key_decay, *extra)


def product_kernel(contract, a_ref, b_ref, *out_refs):
    result = lax.dot_general(
        a_ref[...], b_ref[...], (contract, ((), ())), preferred_element_type=F32
    )
    step = result.shape[0] // len(out_refs)
    for n, out_ref in enumerate(out_refs):
        out_ref[...] = result[n * step : (n + 1) * step].astype(BF16)


def row_product(a, b, transposed, parts, column=0):
    rows, depth = a.shape
    width = b.shape[0] if transposed else b.shape[1]
    tile = min(512, width)
    if transposed:
        b_spec = pl.BlockSpec((tile, depth), lambda n: (n, column))
    else:
        b_spec = pl.BlockSpec((depth, tile), lambda n: (0, n))
    return pl.pallas_call(
        functools.partial(product_kernel, ((1,), (1 if transposed else 0,))),
        grid=(width // tile,),
        in_specs=[pl.BlockSpec((rows, depth), lambda n: (0, 0)), b_spec],
        out_specs=[pl.BlockSpec((rows // parts, tile), lambda n: (0, n))] * parts,
        out_shape=[jax.ShapeDtypeStruct((rows // parts, width), BF16)] * parts,
        compiler_params=pltpu.CompilerParams(vmem_limit_bytes=48 * 1024 * 1024),
        cost_estimate=pl.CostEstimate(
            flops=2 * rows * depth * width,
            bytes_accessed=2 * (rows * depth + depth * width + rows * width),
            transcendentals=0,
        ),
        name="row_product",
    )(a, b)


def feed_kernel(steps, parts, scale_ref, *refs):
    normed_refs, grad_refs = refs[:parts], refs[parts : 2 * parts]
    up_ref, down_ref, up_row_ref, hidden_ref, pre_ref = refs[2 * parts : 2 * parts + 5]
    out_refs, (normed, grad) = refs[2 * parts + 5 : -2], refs[-2:]
    step = pl.program_id(0)

    @pl.when(step == 0)
    def _():
        count = normed_refs[0].shape[0]
        for n in range(parts):
            normed[n * count : (n + 1) * count] = normed_refs[n][...]
            grad[n * count : (n + 1) * count] = (
                grad_refs[n][...].astype(F32) * scale_ref[0]
            ).astype(BF16)

    @pl.when(step < steps)
    def _():
        u = dot(normed[...], up_ref[...])
        d_hidden = dot(grad[...], down_ref[...])
        scale = 0.7978845608028654
        square = u * u
        t = jnp.tanh(scale * u * (1.0 + 0.044715 * square))
        half = 0.5 * (1.0 + t)
        slope = half + 0.5 * scale * u * (1.0 - t * t) * (1.0 + 3 * 0.044715 * square)
        tile = u.shape[1]
        at = pl.ds(pl.multiple_of(step * tile, tile), tile)
        hidden_ref[:, at] = (u * half).astype(BF16)
        pre_ref[:, at] = (d_hidden * slope).astype(BF16)

    @pl.when(step >= steps)
    def _():
        result = contract_cols(pre_ref[...], up_row_ref[...])
        count = result.shape[0] // len(out_refs)
        for n, out_ref in enumerate(out_refs):
            out_ref[...] = result[n * count : (n + 1) * count].astype(BF16)


def feed_call(normed, grad, row_scale, both):
    parts, (count, depth) = len(normed), normed[0].shape
    rows, width = parts * count, both.shape[1] // 2
    tile, out_tile = min(256, width), min(512, depth)
    steps, out_steps = width // tile, depth // out_tile
    first = lambda n: jnp.minimum(n, steps - 1)
    second = lambda n: jnp.maximum(n - steps, 0)
    piece = pl.BlockSpec((count, depth), lambda n: (0, 0), pipeline_mode=pl.Buffered(1))
    whole = pl.BlockSpec((rows, width), lambda n: (0, 0))
    return pl.pallas_call(
        functools.partial(feed_kernel, steps, parts),
        grid=(steps + out_steps,),
        in_specs=[pl.BlockSpec(memory_space=pltpu.SMEM)]
        + [piece] * (2 * parts)
        + [
            pl.BlockSpec((depth, tile), lambda n: (0, first(n))),
            pl.BlockSpec((depth, tile), lambda n: (0, steps + first(n))),
            pl.BlockSpec((out_tile, width), lambda n: (second(n), 0)),
        ],
        out_specs=[whole, whole]
        + [pl.BlockSpec((count, out_tile), lambda n: (0, second(n)))] * parts,
        out_shape=[jax.ShapeDtypeStruct((rows, width), BF16)] * 2
        + [jax.ShapeDtypeStruct((count, depth), BF16)] * parts,
        scratch_shapes=[pltpu.VMEM((rows, depth), BF16)] * 2,
        compiler_params=pltpu.CompilerParams(vmem_limit_bytes=56 * 1024 * 1024),
        cost_estimate=pl.CostEstimate(
            flops=6 * rows * depth * width,
            bytes_accessed=4 * (rows * depth + 2 * depth * width + rows * width),
            transcendentals=rows * width,
        ),
        name="feed_forward",
    )(row_scale.reshape(1), *normed, *grad, both, both, both)


def feed_grads_kernel(parts, scale_ref, *refs):
    normed_refs, grad_refs = refs[:parts], refs[parts : 2 * parts]
    hidden_ref, pre_ref, out_ref, normed, grad = refs[2 * parts :]
    count, width = normed_refs[0].shape[0], hidden_ref.shape[1]
    for n in range(parts):
        normed[n * count : (n + 1) * count] = normed_refs[n][...]
        grad[n * count : (n + 1) * count] = (grad_refs[n][...].astype(F32) * scale_ref[0]).astype(
            BF16
        )
    out_ref[:, :width] = contract_rows(normed[...], pre_ref[...]).astype(BF16)
    out_ref[:, width:] = contract_rows(grad[...], hidden_ref[...]).astype(BF16)


def feed_grads(normed, grad, row_scale, hidden, d_pre):
    parts, (count, depth) = len(normed), normed[0].shape
    rows, width = hidden.shape
    tile = min(512, depth)
    slab = pl.BlockSpec((count, tile), lambda n: (0, n))
    whole = pl.BlockSpec((rows, width), lambda n: (0, 0))
    return pl.pallas_call(
        functools.partial(feed_grads_kernel, parts),
        grid=(depth // tile,),
        in_specs=[pl.BlockSpec(memory_space=pltpu.SMEM)] + [slab] * (2 * parts) + [whole, whole],
        out_specs=pl.BlockSpec((tile, 2 * width), lambda n: (n, 0)),
        out_shape=jax.ShapeDtypeStruct((depth, 2 * width), BF16),
        scratch_shapes=[pltpu.VMEM((rows, tile), BF16)] * 2,
        compiler_params=pltpu.CompilerParams(vmem_limit_bytes=48 * 1024 * 1024),
        cost_estimate=pl.CostEstimate(
            flops=4 * rows * depth * width,
            bytes_accessed=4 * (rows * depth + depth * width + rows * width),
            transcendentals=0,
        ),
        name="feed_grads",
    )(row_scale.reshape(1), *normed, *grad, hidden, d_pre)


def on_device(
    tokens,
    cotangent,
    domain,
    query_weight,
    key_weight,
    value_weight,
    gate_weight,
    output_weight,
    retention_gain,
    retention_bias,
    feedfwd_gain,
    feedfwd_bias,
    up_weight,
    down_weight,
):
    dp, mp = lax.axis_size("dp"), lax.axis_size("mp")
    here = lax.axis_index("mp")
    masks = range(mp)
    rows = tokens.shape[0]
    total = rows * mp
    blocks = total // SPAN
    heads = HEADS // mp
    part = query_weight.shape[0]
    own = part * mp
    square = mp == 4
    parts = 2 * mp if square else mp
    together = lax.optimization_barrier

    def swap(x, mask):
        if mask == 0:
            return x
        return lax.ppermute(x, "mp", [(s, s ^ mask) for s in range(mp)])

    def spread(x):
        return spread_end(spread_start(x))

    def spread_start(x):
        if not square:
            return [swap(x, m) for m in masks]
        half = x.shape[0] // 2
        a, b = x[:half], x[half:]
        a1, b2 = swap(a, 1), swap(b, 2)
        a2, b1 = swap(a, 2), swap(b, 1)
        return [a, b, a1, b1, a2, b2]

    def spread_end(groups):
        if not square:
            return groups
        a1, b2 = groups[2], groups[5]
        return groups + [swap(a1, 2), swap(b2, 1)]

    def collect(pieces, meanwhile=()):
        if not square:
            received = [swap(pieces[m], m) for m in masks[1:]]
            *received, meanwhile = together((*received, meanwhile))
            received = [r.astype(F32) for r in received]
            return functools.reduce(jnp.add, received, pieces[0].astype(F32)), meanwhile
        a0, b0, a1, b1, a2, b2, a3, b3 = pieces
        a3, b3 = swap(a3, 1), swap(b3, 2)
        a1, b2 = swap(a1, 1), swap(b2, 2)
        a3, b3, meanwhile = together((a3, b3, meanwhile))
        a2 = swap((a2.astype(F32) + a3.astype(F32)).astype(BF16), 2)
        b1 = swap((b1.astype(F32) + b3.astype(F32)).astype(BF16), 1)
        total = jnp.concatenate(
            [
                a0.astype(F32) + a1.astype(F32) + a2.astype(F32),
                b0.astype(F32) + b1.astype(F32) + b2.astype(F32),
            ],
            axis=0,
        )
        return total, meanwhile

    def gather_start(x):
        if dp != 8:
            return (x,), lambda arrived, meanwhile: (
                lax.all_gather(arrived[0], "dp", axis=0, tiled=True),
                meanwhile,
            )
        index = lax.axis_index("dp")
        core, place = index % 2, index // 2
        move = lambda v, pairs: lax.ppermute(
            v, "dp", [(2 * s + c, 2 * d + c) for s, d in pairs for c in range(2)]
        )
        above = move(x, [(1, 0), (2, 1), (3, 2)])
        below = move(x, [(0, 1), (1, 2), (2, 3)])
        across = move(x, [(0, 3), (3, 0)])

        def finish(arrived, meanwhile):
            above, below, across = arrived
            onward = jnp.where(place == 1, above, jnp.where(place == 2, below, x))
            over = move(onward, [(0, 2), (3, 1), (2, 3), (1, 0)])
            over, meanwhile = together((over, meanwhile))
            by_place = []
            for k in range(4):
                apart = place - k
                far = jnp.where(abs(apart) == 3, across, over)
                near = jnp.where(apart == 1, below, jnp.where(apart == -1, above, far))
                by_place.append(jnp.where(apart == 0, x, near))
            mine = jnp.stack(by_place)
            other = lax.ppermute(mine, "dp", [(s, s ^ 1) for s in range(dp)])
            both = [jnp.where(core == 0, mine, other), jnp.where(core == 0, other, mine)]
            return jnp.stack(both, axis=1).reshape(dp * x.shape[0], x.shape[1]), meanwhile

        return (above, below, across), finish

    def scatter_small(x):
        cur = x.reshape(dp, mp, x.shape[-1])
        for dim, name in ((1, "mp"), (0, "dp")):
            index = lax.axis_index(name)
            while cur.shape[dim] > 1:
                count = cur.shape[dim] // 2
                bit = (index // count) % 2
                mine = lax.dynamic_slice_in_dim(cur, bit * count, count, dim)
                other = lax.dynamic_slice_in_dim(cur, (1 - bit) * count, count, dim)
                pairs = [(s, s ^ count) for s in range(lax.axis_size(name))]
                cur = mine + lax.ppermute(other, name, pairs)
        return cur.reshape(-1)

    def by_index(pieces):
        stacked = jnp.stack(pieces)
        return [
            lax.dynamic_index_in_dim(stacked, here ^ m, 0, keepdims=False) for m in masks
        ]

    thin = jnp.concatenate(
        [retention_gain, retention_bias, feedfwd_gain, feedfwd_bias]
        + [jnp.broadcast_to(domain.astype(BF16), (part,))]
    )
    strip, thin_size = output_weight.shape[0], thin.shape[0]
    thin = jnp.pad(thin[None], ((0, 15), (0, output_weight.shape[1] - thin_size)))
    def columns(weight, target):
        width = weight.shape[1] // mp
        return lax.dynamic_slice(weight, (0, target * width), (part, width))

    pieces = []
    for m in masks:
        target = here ^ m
        pieces.append(
            jnp.concatenate(
                [columns(w, target) for w in (query_weight, key_weight, value_weight, gate_weight)],
                axis=1,
            )
        )
    pieces, output_weight, thin = together((pieces, output_weight, thin))
    pieces = [swap(pieces[m], m) for m in masks]
    arrived, finish = gather_start(jnp.concatenate([output_weight, thin], axis=0))
    pieces, arrived = together((pieces, arrived))
    packed = jnp.concatenate(by_index(pieces), axis=0)
    w_in = lax.all_gather(packed, "dp", axis=0, tiled=True)
    tokens_late, packed = together((tokens, packed))
    w_out, source_rows = finish(arrived, spread_start(tokens_late))
    source_rows = spread_end(source_rows)
    w_out = w_out.reshape(dp, strip + 16, -1)
    thin = w_out[:, strip, :thin_size]
    w_out = w_out[:, :strip].reshape(dp * strip, -1)
    thin = jnp.stack(by_index([swap(thin, m) for m in masks]))
    thin = thin.reshape(mp, dp, 5, part).transpose(2, 1, 0, 3).reshape(5, dp * own)
    gain_one, bias_one, gain_two, bias_two = (thin[n].astype(F32)[None] for n in range(4))

    w_out, *source_rows = together((w_out, *source_rows))
    group = w_out.shape[0] // mp
    w_out = [
        lax.dynamic_slice_in_dim(w_out, (here ^ m) * group, group, 0) for m in masks
    ]
    w_out = by_index([swap(w_out[m], m) for m in masks])
    cotangent_late, *w_out = together((cotangent, *w_out))
    cotan_rows = spread(cotangent_late)
    w_out = jnp.stack([w.reshape(group // strip, strip, -1) for w in w_out], axis=1)
    w_out = w_out.reshape(group * mp, -1)

    domains = thin[4, ::own]
    own_count = jnp.sum((domains == domain[0].astype(BF16)).astype(F32)) * (rows * mp)
    row_scale = F32(rows * dp * mp) / (DOMAINS * own_count)

    tables = rotation_tables(total, KHEAD)
    decay = decays(heads, here * heads)
    block_order = (
        (jnp.arange(mp, dtype=jnp.int32) ^ here)[:, None] * (rows // SPAN)
        + jnp.arange(rows // SPAN, dtype=jnp.int32)[None]
    ).reshape(-1)

    normal_rows, _ = layer_stats(jnp.concatenate(source_rows, axis=0).astype(F32))
    normed_one = (normal_rows * gain_one + bias_one).astype(BF16)
    normed_one, tables, decay, w_out = together((normed_one, tables, decay, w_out))
    w_feed = lax.all_gather(
        jnp.concatenate([up_weight, down_weight.T], axis=1), "dp", axis=0, tiled=True
    )

    pre = dot(normed_one, w_in)
    gated, state_low = retention_call(heads, blocks, block_order, pre, tables, decay, ())

    gated, cotan_rows = together((gated, cotan_rows))
    source = tokens.astype(F32)
    middle = source + collect(row_product(gated, w_out, False, parts))[0]
    normal_two, factor_two = layer_stats(middle)
    normed_two = (normal_two * gain_two + bias_two).astype(BF16)
    normed_rows = spread(normed_two)
    hidden, d_pre, *pieces = feed_call(normed_rows, cotan_rows, row_scale, w_feed)
    *pieces, hidden, d_pre = together((*pieces, hidden, d_pre))
    feed_part = feed_grads(normed_rows, cotan_rows, row_scale, hidden, d_pre)
    d_normed_two, feed_part = collect(pieces, feed_part)
    scatter = functools.partial(
        lax.psum_scatter, axis_name="dp", scatter_dimension=0, tiled=True
    )
    feed_grad = scatter(feed_part)

    cotan = cotangent.astype(F32) * row_scale
    d_middle = cotan + layer_back(d_normed_two * gain_two, normal_two, factor_two)
    branch_rows = jnp.concatenate(spread(d_middle.astype(BF16)), axis=0)
    d_gated = contract_cols(branch_rows, w_out)
    d_in = retention_call(
        heads, blocks, block_order, pre, tables, decay, (state_low, d_gated)
    )
    in_part = contract_rows(normed_one, d_in).astype(BF16)
    in_part, gated, feed_grad = together((in_part, gated, feed_grad))
    in_grad = scatter(in_part)
    output_part = contract_rows(gated, branch_rows).astype(BF16)
    output_part = output_part.reshape(group // strip, mp, strip, -1)
    pieces = [
        lax.dynamic_index_in_dim(output_part, here ^ m, 1, keepdims=False).reshape(group, -1)
        for m in masks
    ]
    *pieces, d_in = together((*pieces, d_in))
    output_pieces = [swap(pieces[m], m) for m in masks]
    *pieces, hidden = together((*row_product(d_in, w_in, True, parts), hidden))
    feed_pieces = row_product(hidden, w_feed, True, parts, 1)
    output_pieces, pieces, feed_pieces = together((output_pieces, pieces, feed_pieces))
    output_part = jnp.concatenate(by_index(output_pieces), axis=0)
    d_normed_one, output_part = collect(pieces, output_part)
    d_normed_one, feed_pieces = together((d_normed_one, feed_pieces))
    normal_one, factor_one = layer_stats(source)
    d_tokens = d_middle + layer_back(d_normed_one * gain_one, normal_one, factor_one)

    feed_sum, _ = collect(feed_pieces)
    outputs = (middle + feed_sum).astype(BF16)

    width = up_weight.shape[1]
    up_grad = feed_grad[:, :width].astype(F32)
    down_grad = feed_grad[:, width:].astype(F32).T
    output_part, in_grad, outputs, d_tokens = together((output_part, in_grad, outputs, d_tokens))
    output_grad = scatter(output_part).astype(F32)
    pieces = by_index([in_grad[m * part : (m + 1) * part] for m in masks])
    pieces = by_index([swap(pieces[m], m) for m in masks])
    grads, at = [], 0
    for weight in (query_weight, key_weight, value_weight, gate_weight):
        width = weight.shape[1] // mp
        grads.append(
            jnp.concatenate([p[:, at : at + width] for p in pieces], axis=1).astype(F32)
        )
        at += width

    thin_grads = jnp.stack(
        [
            jnp.sum(d_normed_one * normal_one, axis=0),
            jnp.sum(d_normed_one, axis=0),
            jnp.sum(d_normed_two * normal_two, axis=0),
            jnp.sum(d_normed_two, axis=0),
        ],
        axis=0,
    )
    thin_grads = thin_grads.reshape(4, dp * mp, part).transpose(1, 0, 2).reshape(dp * mp, 4 * part)
    thin_grads = scatter_small(thin_grads).reshape(4, part)
    return (
        outputs,
        d_tokens.astype(BF16),
        *grads,
        output_grad,
        *(thin_grads[n] for n in range(4)),
        up_grad,
        down_grad,
    )


def solution(mesh):
    return jax.shard_map(
        on_device,
        mesh=mesh,
        in_specs=(
            P(("dp", "mp"), None),
            P(("dp", "mp"), None),
            P("dp"),
            P(("dp", "mp"), None),
            P(("dp", "mp"), None),
            P(("dp", "mp"), None),
            P(("dp", "mp"), None),
            P(("dp", "mp"), None),
            P(("dp", "mp")),
            P(("dp", "mp")),
            P(("dp", "mp")),
            P(("dp", "mp")),
            P("dp", "mp"),
            P("mp", "dp"),
        ),
        out_specs=(
            P(("dp", "mp"), None),
            P(("dp", "mp"), None),
            P(("dp", "mp"), None),
            P(("dp", "mp"), None),
            P(("dp", "mp"), None),
            P(("dp", "mp"), None),
            P(("dp", "mp"), None),
            P(("dp", "mp")),
            P(("dp", "mp")),
            P(("dp", "mp")),
            P(("dp", "mp")),
            P("dp", "mp"),
            P("mp", "dp"),
        ),
        check_vma=False,
    )
```

```python
import functools

import jax
import jax.numpy as jnp
from jax import lax
from jax.experimental import pallas as pl
from jax.experimental.pallas import tpu as pltpu
from jax.sharding import PartitionSpec as P

D = 2048
DV = 4096
HEADS = 8
KHEAD = 256
VHEAD = 512
SPAN = 256
DOMAINS = 4


EPSILON = 1e-05
F32 = jnp.float32
BF16 = jnp.bfloat16


def layer_stats(values):
    center = values - jnp.mean(values, axis=-1, keepdims=True)
    factor = lax.rsqrt(jnp.mean(center * center, axis=-1, keepdims=True) + EPSILON)
    return (center * factor, factor)


def layer_back(grad, normal, factor):
    return factor * (
        grad
        - jnp.mean(grad, axis=-1, keepdims=True)
        - normal * jnp.mean(grad * normal, axis=-1, keepdims=True)
    )


def decay_logs(heads):
    return jnp.log1p(-jnp.exp2(-5.0 - jnp.arange(heads, dtype=jnp.float32)))


def rotation_tables(count, width):
    freq = 10000.0 ** (-2.0 * jnp.arange(width // 2, dtype=jnp.float32) / width)
    places = jnp.arange(count, dtype=jnp.int32).astype(jnp.float32)
    angle = places[:, None] * freq[None, :]
    return (jnp.cos(angle), jnp.sin(angle))


def dot(left, right):
    return jnp.dot(left, right, preferred_element_type=F32)


def contract_rows(left, right):
    return lax.dot_general(
        left, right, (((0,), (0,)), ((), ())), preferred_element_type=F32
    )


def contract_cols(left, right):
    return lax.dot_general(
        left, right, (((1,), (1,)), ((), ())), preferred_element_type=F32
    )


def rotate(values, cosine, sine):
    half = values.shape[-1] // 2
    first, second = values[:, :half], values[:, half:]
    return jnp.concatenate(
        [first * cosine - second * sine, first * sine + second * cosine], axis=-1
    )


def unrotate(values, cosine, sine):
    half = values.shape[-1] // 2
    first, second = values[:, :half], values[:, half:]
    return jnp.concatenate(
        [first * cosine + second * sine, second * cosine - first * sine], axis=-1
    )


def head_forward(h, heads, pre_ref, cosine, sine, inner_decay, place_decay, state_low):
    q_at, k_at = h * KHEAD, (heads + h) * KHEAD
    v_at, g_at = 2 * heads * KHEAD + h * VHEAD, 2 * heads * KHEAD + (heads + h) * VHEAD
    query = rotate(pre_ref[:, q_at : q_at + KHEAD], cosine, sine).astype(BF16)
    key = rotate(pre_ref[:, k_at : k_at + KHEAD], cosine, sine).astype(BF16)
    value = pre_ref[:, v_at : v_at + VHEAD].astype(BF16)
    gate = pre_ref[:, g_at : g_at + VHEAD]
    weights = (contract_cols(query, key) * inner_decay).astype(BF16)
    retained = dot(weights, value) + dot(query, state_low) * place_decay
    grouped, factor = layer_stats(retained)
    return query, key, value, gate, weights, grouped, factor


def retention_forward_kernel(
    heads, order_ref, block_ref, pre_ref, cos_ref, sin_ref, inner_ref, place_ref, key_ref,
    gated_ref, low_ref, state,
):
    @pl.when(pl.program_id(0) == 0)
    def _():
        state[...] = jnp.zeros_like(state)

    cosine, sine = cos_ref[...], sin_ref[...]
    for h in range(heads):
        before = state[h]
        state_low = before.astype(BF16)
        low_ref[0, h] = state_low
        query, key, value, gate, weights, grouped, factor = head_forward(
            h, heads, pre_ref, cosine, sine, inner_ref[h], place_ref[h], state_low
        )
        gated = gate * jax.nn.sigmoid(gate) * grouped
        gated_ref[:, h * VHEAD : (h + 1) * VHEAD] = gated.astype(BF16)
        key_scaled = (key.astype(F32) * key_ref[h]).astype(BF16)
        state[h] = before * block_ref[h] + contract_rows(key_scaled, value)


def retention_backward_kernel(
    heads, order_ref, block_ref, pre_ref, cos_ref, sin_ref, inner_ref, place_ref, key_ref,
    low_ref, grad_ref, out_ref, state,
):
    @pl.when(pl.program_id(0) == 0)
    def _():
        state[...] = jnp.zeros_like(state)

    cosine, sine = cos_ref[...], sin_ref[...]
    for h in range(heads):
        state_low = low_ref[0, h]
        inner_decay, place_decay, key_decay = inner_ref[h], place_ref[h], key_ref[h]
        query, key, value, gate, weights, grouped, factor = head_forward(
            h, heads, pre_ref, cosine, sine, inner_decay, place_decay, state_low
        )
        q_at, k_at = h * KHEAD, (heads + h) * KHEAD
        v_at, g_at = 2 * heads * KHEAD + h * VHEAD, 2 * heads * KHEAD + (heads + h) * VHEAD
        d_gated = grad_ref[:, h * VHEAD : (h + 1) * VHEAD]
        sigma = jax.nn.sigmoid(gate)
        swish = gate * sigma
        out_ref[:, g_at : g_at + VHEAD] = (
            d_gated * grouped * (sigma + swish * (1.0 - sigma))
        ).astype(BF16)
        d_retained = layer_back(d_gated * swish, grouped, factor)
        d_inner = d_retained.astype(BF16)
        d_carried = (d_retained * place_decay).astype(BF16)
        d_scores = (contract_cols(d_inner, value) * inner_decay).astype(BF16)
        after = state[h]
        local_grad = after.astype(BF16)
        key_scaled = (key.astype(F32) * key_decay).astype(BF16)
        d_query = dot(d_scores, key) + contract_cols(d_carried, state_low)
        d_key = contract_rows(d_scores, query) + key_decay * contract_cols(value, local_grad)
        d_value = contract_rows(weights, d_inner) + dot(key_scaled, local_grad)
        out_ref[:, q_at : q_at + KHEAD] = unrotate(d_query, cosine, sine).astype(BF16)
        out_ref[:, k_at : k_at + KHEAD] = unrotate(d_key, cosine, sine).astype(BF16)
        out_ref[:, v_at : v_at + VHEAD] = d_value.astype(BF16)
        state[h] = after * block_ref[h] + contract_rows(query, d_carried)


def decays(heads, first):
    logs = lax.dynamic_slice(decay_logs(HEADS), (first,), (heads,))
    places = jnp.arange(SPAN, dtype=F32)
    spacing = places[:, None] - places[None, :]
    inner = jnp.where(
        spacing[None] >= 0, jnp.exp(jnp.maximum(spacing, 0.0)[None] * logs[:, None, None]), 0.0
    )
    place = jnp.exp(places[None, :] * logs[:, None])[:, :, None]
    key = jnp.exp((SPAN - places)[None, :] * logs[:, None])[:, :, None]
    return inner, place, key, jnp.exp(SPAN * logs)


def retention_call(heads, blocks, order, pre, tables, decay, extra):
    backward = bool(extra)
    wide, narrow = pre.shape[1], heads * VHEAD
    at = (lambda t: blocks - 1 - t) if backward else (lambda t: t)
    row = lambda t, order, *_: (order[at(t)], 0)
    place = lambda t, *_: (at(t), 0)
    whole = lambda t, *_: (0, 0, 0)
    low_spec = pl.BlockSpec((1, heads, KHEAD, VHEAD), lambda t, *_: (at(t), 0, 0, 0))
    in_specs = [
        pl.BlockSpec((SPAN, wide), row),
        pl.BlockSpec((SPAN, KHEAD // 2), place),
        pl.BlockSpec((SPAN, KHEAD // 2), place),
        pl.BlockSpec((heads, SPAN, SPAN), whole),
        pl.BlockSpec((heads, SPAN, 1), whole),
        pl.BlockSpec((heads, SPAN, 1), whole),
    ]
    inner, place_decay, key_decay, block_decay = decay
    if backward:
        in_specs += [low_spec, pl.BlockSpec((SPAN, narrow), row)]
        out_specs = pl.BlockSpec((SPAN, wide), row)
        out_shape = jax.ShapeDtypeStruct(pre.shape, BF16)
        body = retention_backward_kernel
    else:
        out_specs = (pl.BlockSpec((SPAN, narrow), row), low_spec)
        out_shape = (
            jax.ShapeDtypeStruct((pre.shape[0], narrow), BF16),
            jax.ShapeDtypeStruct((blocks, heads, KHEAD, VHEAD), BF16),
        )
        body = retention_forward_kernel
    products = (15 if backward else 7) * SPAN * SPAN * SPAN * 2 * heads * blocks
    return pl.pallas_call(
        functools.partial(body, heads),
        grid_spec=pltpu.PrefetchScalarGridSpec(
            num_scalar_prefetch=2,
            grid=(blocks,),
            in_specs=in_specs,
            out_specs=out_specs,
            scratch_shapes=[pltpu.VMEM((heads, KHEAD, VHEAD), F32)],
        ),
        out_shape=out_shape,
        compiler_params=pltpu.CompilerParams(vmem_limit_bytes=48 * 1024 * 1024),
        cost_estimate=pl.CostEstimate(
            flops=products, bytes_accessed=pre.size * (6 if backward else 5), transcendentals=0
        ),
        name="retention_backward" if backward else "retention_forward",
    )(order, block_decay, pre, *tables, inner, place_decay, key_decay, *extra)


def product_kernel(contract, a_ref, b_ref, *out_refs):
    result = lax.dot_general(
        a_ref[...], b_ref[...], (contract, ((), ())), preferred_element_type=F32
    )
    step = result.shape[0] // len(out_refs)
    for n, out_ref in enumerate(out_refs):
        out_ref[...] = result[n * step : (n + 1) * step].astype(BF16)


def row_product(a, b, transposed, parts, column=0):
    rows, depth = a.shape
    width = b.shape[0] if transposed else b.shape[1]
    tile = min(512, width)
    if transposed:
        b_spec = pl.BlockSpec((tile, depth), lambda n: (n, column))
    else:
        b_spec = pl.BlockSpec((depth, tile), lambda n: (0, n))
    return pl.pallas_call(
        functools.partial(product_kernel, ((1,), (1 if transposed else 0,))),
        grid=(width // tile,),
        in_specs=[pl.BlockSpec((rows, depth), lambda n: (0, 0)), b_spec],
        out_specs=[pl.BlockSpec((rows // parts, tile), lambda n: (0, n))] * parts,
        out_shape=[jax.ShapeDtypeStruct((rows // parts, width), BF16)] * parts,
        compiler_params=pltpu.CompilerParams(vmem_limit_bytes=48 * 1024 * 1024),
        cost_estimate=pl.CostEstimate(
            flops=2 * rows * depth * width,
            bytes_accessed=2 * (rows * depth + depth * width + rows * width),
            transcendentals=0,
        ),
        name="row_product",
    )(a, b)


def feed_before_kernel(parts, scale_ref, *refs):
    grad_refs, (down_ref, hidden_ref, grad_ref) = refs[:parts], refs[parts:]

    @pl.when(pl.program_id(0) == 0)
    def _():
        count = grad_refs[0].shape[0]
        for n in range(parts):
            grad_ref[n * count : (n + 1) * count] = (
                grad_refs[n][...].astype(F32) * scale_ref[0]
            ).astype(BF16)

    hidden_ref[...] = dot(grad_ref[...], down_ref[...])


def feed_before(grad, row_scale, both):
    parts, (count, depth) = len(grad), grad[0].shape
    rows, width = parts * count, both.shape[1] // 2
    tile = min(256, width)
    steps = width // tile
    piece = pl.BlockSpec((count, depth), lambda n: (0, 0), pipeline_mode=pl.Buffered(1))
    return pl.pallas_call(
        functools.partial(feed_before_kernel, parts),
        grid=(steps,),
        in_specs=[pl.BlockSpec(memory_space=pltpu.SMEM)]
        + [piece] * parts
        + [pl.BlockSpec((depth, tile), lambda n: (0, steps + n))],
        out_specs=[
            pl.BlockSpec((rows, tile), lambda n: (0, n)),
            pl.BlockSpec((rows, depth), lambda n: (0, 0)),
        ],
        out_shape=[
            jax.ShapeDtypeStruct((rows, width), F32),
            jax.ShapeDtypeStruct((rows, depth), BF16),
        ],
        compiler_params=pltpu.CompilerParams(vmem_limit_bytes=48 * 1024 * 1024),
        cost_estimate=pl.CostEstimate(
            flops=2 * rows * depth * width,
            bytes_accessed=4 * (rows * depth + depth * width + rows * width),
            transcendentals=0,
        ),
        name="feed_before",
    )(row_scale.reshape(1), *grad, both)


def feed_kernel(steps, parts, *refs):
    normed_refs = refs[:parts]
    d_hidden_ref, up_ref, up_row_ref, hidden_ref, pre_ref = refs[parts : parts + 5]
    out_refs, normed = refs[parts + 5 : -1], refs[-1]
    step = pl.program_id(0)

    @pl.when(step == 0)
    def _():
        count = normed_refs[0].shape[0]
        for n in range(parts):
            normed[n * count : (n + 1) * count] = normed_refs[n][...]

    @pl.when(step < steps)
    def _():
        u = dot(normed[...], up_ref[...])
        scale = 0.7978845608028654
        square = u * u
        t = jnp.tanh(scale * u * (1.0 + 0.044715 * square))
        half = 0.5 * (1.0 + t)
        slope = half + 0.5 * scale * u * (1.0 - t * t) * (1.0 + 3 * 0.044715 * square)
        tile = u.shape[1]
        at = pl.ds(pl.multiple_of(step * tile, tile), tile)
        hidden_ref[:, at] = (u * half).astype(BF16)
        pre_ref[:, at] = (d_hidden_ref[...] * slope).astype(BF16)

    @pl.when(step >= steps)
    def _():
        result = contract_cols(pre_ref[...], up_row_ref[...])
        count = result.shape[0] // len(out_refs)
        for n, out_ref in enumerate(out_refs):
            out_ref[...] = result[n * count : (n + 1) * count].astype(BF16)


def feed_call(normed, d_hidden, both):
    parts, (count, depth) = len(normed), normed[0].shape
    rows, width = d_hidden.shape
    tile, out_tile = min(256, width), min(512, depth)
    steps, out_steps = width // tile, depth // out_tile
    first = lambda n: jnp.minimum(n, steps - 1)
    second = lambda n: jnp.maximum(n - steps, 0)
    piece = pl.BlockSpec((count, depth), lambda n: (0, 0), pipeline_mode=pl.Buffered(1))
    whole = pl.BlockSpec((rows, width), lambda n: (0, 0))
    return pl.pallas_call(
        functools.partial(feed_kernel, steps, parts),
        grid=(steps + out_steps,),
        in_specs=[piece] * parts
        + [
            pl.BlockSpec((rows, tile), lambda n: (0, first(n))),
            pl.BlockSpec((depth, tile), lambda n: (0, first(n))),
            pl.BlockSpec((out_tile, width), lambda n: (second(n), 0)),
        ],
        out_specs=[whole, whole]
        + [pl.BlockSpec((count, out_tile), lambda n: (0, second(n)))] * parts,
        out_shape=[jax.ShapeDtypeStruct((rows, width), BF16)] * 2
        + [jax.ShapeDtypeStruct((count, depth), BF16)] * parts,
        scratch_shapes=[pltpu.VMEM((rows, depth), BF16)],
        compiler_params=pltpu.CompilerParams(vmem_limit_bytes=58 * 1024 * 1024),
        cost_estimate=pl.CostEstimate(
            flops=4 * rows * depth * width,
            bytes_accessed=2 * (3 * rows * depth + 2 * depth * width + rows * width),
            transcendentals=rows * width,
        ),
        name="feed_forward",
    )(*normed, d_hidden, both, both)


def feed_grads_kernel(parts, *refs):
    normed_refs, (grad_ref, hidden_ref, pre_ref, out_ref, normed) = refs[:parts], refs[parts:]
    count, width = normed_refs[0].shape[0], hidden_ref.shape[1]
    for n in range(parts):
        normed[n * count : (n + 1) * count] = normed_refs[n][...]
    out_ref[:, :width] = contract_rows(normed[...], pre_ref[...]).astype(BF16)
    out_ref[:, width:] = contract_rows(grad_ref[...], hidden_ref[...]).astype(BF16)


def feed_grads(normed, grad, hidden, d_pre):
    parts, (count, depth) = len(normed), normed[0].shape
    rows, width = hidden.shape
    tile = min(512, depth)
    whole = pl.BlockSpec((rows, width), lambda n: (0, 0))
    return pl.pallas_call(
        functools.partial(feed_grads_kernel, parts),
        grid=(depth // tile,),
        in_specs=[pl.BlockSpec((count, tile), lambda n: (0, n))] * parts
        + [pl.BlockSpec((rows, tile), lambda n: (0, n)), whole, whole],
        out_specs=pl.BlockSpec((tile, 2 * width), lambda n: (n, 0)),
        out_shape=jax.ShapeDtypeStruct((depth, 2 * width), BF16),
        scratch_shapes=[pltpu.VMEM((rows, tile), BF16)],
        compiler_params=pltpu.CompilerParams(vmem_limit_bytes=48 * 1024 * 1024),
        cost_estimate=pl.CostEstimate(
            flops=4 * rows * depth * width,
            bytes_accessed=4 * (rows * depth + depth * width + rows * width),
            transcendentals=0,
        ),
        name="feed_grads",
    )(*normed, grad, hidden, d_pre)


def on_device(
    tokens,
    cotangent,
    domain,
    query_weight,
    key_weight,
    value_weight,
    gate_weight,
    output_weight,
    retention_gain,
    retention_bias,
    feedfwd_gain,
    feedfwd_bias,
    up_weight,
    down_weight,
):
    dp, mp = lax.axis_size("dp"), lax.axis_size("mp")
    here = lax.axis_index("mp")
    masks = range(mp)
    rows = tokens.shape[0]
    total = rows * mp
    blocks = total // SPAN
    heads = HEADS // mp
    part = query_weight.shape[0]
    own = part * mp
    square = mp == 4
    parts = 2 * mp if square else mp
    together = lax.optimization_barrier

    def swap(x, mask):
        if mask == 0:
            return x
        return lax.ppermute(x, "mp", [(s, s ^ mask) for s in range(mp)])

    def spread(x):
        return spread_end(spread_start(x))

    def spread_start(x):
        if not square:
            return [swap(x, m) for m in masks]
        half = x.shape[0] // 2
        a, b = x[:half], x[half:]
        a1, b2 = swap(a, 1), swap(b, 2)
        a2, b1 = swap(a, 2), swap(b, 1)
        return [a, b, a1, b1, a2, b2]

    def spread_end(groups):
        if not square:
            return groups
        a1, b2 = groups[2], groups[5]
        return groups + [swap(a1, 2), swap(b2, 1)]

    def collect(pieces, meanwhile=()):
        if not square:
            received = [swap(pieces[m], m) for m in masks[1:]]
            *received, meanwhile = together((*received, meanwhile))
            received = [r.astype(F32) for r in received]
            return functools.reduce(jnp.add, received, pieces[0].astype(F32)), meanwhile
        a0, b0, a1, b1, a2, b2, a3, b3 = pieces
        a3, b3 = swap(a3, 1), swap(b3, 2)
        a1, b2 = swap(a1, 1), swap(b2, 2)
        a3, b3, meanwhile = together((a3, b3, meanwhile))
        a2 = swap((a2.astype(F32) + a3.astype(F32)).astype(BF16), 2)
        b1 = swap((b1.astype(F32) + b3.astype(F32)).astype(BF16), 1)
        total = jnp.concatenate(
            [
                a0.astype(F32) + a1.astype(F32) + a2.astype(F32),
                b0.astype(F32) + b1.astype(F32) + b2.astype(F32),
            ],
            axis=0,
        )
        return total, meanwhile

    def gather_start(x):
        if dp != 8:
            return (x,), lambda arrived, meanwhile: (
                lax.all_gather(arrived[0], "dp", axis=0, tiled=True),
                meanwhile,
            )
        index = lax.axis_index("dp")
        core, place = index % 2, index // 2
        move = lambda v, pairs: lax.ppermute(
            v, "dp", [(2 * s + c, 2 * d + c) for s, d in pairs for c in range(2)]
        )
        above = move(x, [(1, 0), (2, 1), (3, 2)])
        below = move(x, [(0, 1), (1, 2), (2, 3)])
        across = move(x, [(0, 3), (3, 0)])

        def finish(arrived, meanwhile):
            above, below, across = arrived
            onward = jnp.where(place == 1, above, jnp.where(place == 2, below, x))
            over = move(onward, [(0, 2), (3, 1), (2, 3), (1, 0)])
            over, meanwhile = together((over, meanwhile))
            by_place = []
            for k in range(4):
                apart = place - k
                far = jnp.where(abs(apart) == 3, across, over)
                near = jnp.where(apart == 1, below, jnp.where(apart == -1, above, far))
                by_place.append(jnp.where(apart == 0, x, near))
            mine = jnp.stack(by_place)
            other = lax.ppermute(mine, "dp", [(s, s ^ 1) for s in range(dp)])
            both = [jnp.where(core == 0, mine, other), jnp.where(core == 0, other, mine)]
            return jnp.stack(both, axis=1).reshape(dp * x.shape[0], x.shape[1]), meanwhile

        return (above, below, across), finish

    def scatter_small(x):
        cur = x.reshape(dp, mp, x.shape[-1])
        for dim, name in ((1, "mp"), (0, "dp")):
            index = lax.axis_index(name)
            while cur.shape[dim] > 1:
                count = cur.shape[dim] // 2
                bit = (index // count) % 2
                mine = lax.dynamic_slice_in_dim(cur, bit * count, count, dim)
                other = lax.dynamic_slice_in_dim(cur, (1 - bit) * count, count, dim)
                pairs = [(s, s ^ count) for s in range(lax.axis_size(name))]
                cur = mine + lax.ppermute(other, name, pairs)
        return cur.reshape(-1)

    def by_index(pieces):
        stacked = jnp.stack(pieces)
        return [
            lax.dynamic_index_in_dim(stacked, here ^ m, 0, keepdims=False) for m in masks
        ]

    thin = jnp.concatenate(
        [retention_gain, retention_bias, feedfwd_gain, feedfwd_bias]
        + [jnp.broadcast_to(domain.astype(BF16), (part,))]
    )
    strip, thin_size = output_weight.shape[0], thin.shape[0]
    thin = jnp.pad(thin[None], ((0, 15), (0, output_weight.shape[1] - thin_size)))
    def columns(weight, target):
        width = weight.shape[1] // mp
        return lax.dynamic_slice(weight, (0, target * width), (part, width))

    pieces = []
    for m in masks:
        target = here ^ m
        pieces.append(
            jnp.concatenate(
                [columns(w, target) for w in (query_weight, key_weight, value_weight, gate_weight)],
                axis=1,
            )
        )
    pieces, output_weight, thin = together((pieces, output_weight, thin))
    pieces = [swap(pieces[m], m) for m in masks]
    arrived, finish = gather_start(jnp.concatenate([output_weight, thin], axis=0))
    pieces, arrived = together((pieces, arrived))
    packed = jnp.concatenate(by_index(pieces), axis=0)
    w_in = lax.all_gather(packed, "dp", axis=0, tiled=True)
    tokens_late, packed = together((tokens, packed))
    w_out, source_rows = finish(arrived, spread_start(tokens_late))
    source_rows = spread_end(source_rows)
    w_out = w_out.reshape(dp, strip + 16, -1)
    thin = w_out[:, strip, :thin_size]
    w_out = w_out[:, :strip].reshape(dp * strip, -1)
    thin = jnp.stack(by_index([swap(thin, m) for m in masks]))
    thin = thin.reshape(mp, dp, 5, part).transpose(2, 1, 0, 3).reshape(5, dp * own)
    gain_one, bias_one, gain_two, bias_two = (thin[n].astype(F32)[None] for n in range(4))

    w_out, *source_rows = together((w_out, *source_rows))
    group = w_out.shape[0] // mp
    w_out = [
        lax.dynamic_slice_in_dim(w_out, (here ^ m) * group, group, 0) for m in masks
    ]
    w_out = by_index([swap(w_out[m], m) for m in masks])
    cotangent_late, *w_out = together((cotangent, *w_out))
    cotan_rows = spread(cotangent_late)
    w_out = jnp.stack([w.reshape(group // strip, strip, -1) for w in w_out], axis=1)
    w_out = w_out.reshape(group * mp, -1)

    domains = thin[4, ::own]
    own_count = jnp.sum((domains == domain[0].astype(BF16)).astype(F32)) * (rows * mp)
    row_scale = F32(rows * dp * mp) / (DOMAINS * own_count)

    tables = rotation_tables(total, KHEAD)
    decay = decays(heads, here * heads)
    block_order = (
        (jnp.arange(mp, dtype=jnp.int32) ^ here)[:, None] * (rows // SPAN)
        + jnp.arange(rows // SPAN, dtype=jnp.int32)[None]
    ).reshape(-1)

    normal_rows, _ = layer_stats(jnp.concatenate(source_rows, axis=0).astype(F32))
    normed_one = (normal_rows * gain_one + bias_one).astype(BF16)
    normed_one, tables, decay, w_out = together((normed_one, tables, decay, w_out))
    w_feed = lax.all_gather(
        jnp.concatenate([up_weight, down_weight.T], axis=1), "dp", axis=0, tiled=True
    )

    pre = dot(normed_one, w_in)
    gated, state_low = retention_call(heads, blocks, block_order, pre, tables, decay, ())

    gated, cotan_rows = together((gated, cotan_rows))
    source = tokens.astype(F32)
    middle = source + collect(row_product(gated, w_out, False, parts))[0]
    normal_two, factor_two = layer_stats(middle)
    normed_two = (normal_two * gain_two + bias_two).astype(BF16)
    normed_rows = spread_start(normed_two)
    d_hidden, grad_rows = feed_before(cotan_rows, row_scale, w_feed)
    normed_rows, d_hidden = together((normed_rows, d_hidden))
    normed_rows = spread_end(normed_rows)
    hidden, d_pre, *pieces = feed_call(normed_rows, d_hidden, w_feed)
    *pieces, hidden, d_pre = together((*pieces, hidden, d_pre))
    feed_part = feed_grads(normed_rows, grad_rows, hidden, d_pre)
    d_normed_two, feed_part = collect(pieces, feed_part)
    scatter = functools.partial(
        lax.psum_scatter, axis_name="dp", scatter_dimension=0, tiled=True
    )
    feed_grad = scatter(feed_part)

    cotan = cotangent.astype(F32) * row_scale
    d_middle = cotan + layer_back(d_normed_two * gain_two, normal_two, factor_two)
    branch_rows = jnp.concatenate(spread(d_middle.astype(BF16)), axis=0)
    d_gated = contract_cols(branch_rows, w_out)
    d_in = retention_call(
        heads, blocks, block_order, pre, tables, decay, (state_low, d_gated)
    )
    in_part = contract_rows(normed_one, d_in).astype(BF16)
    in_part, gated, feed_grad = together((in_part, gated, feed_grad))
    in_grad = scatter(in_part)
    output_part = contract_rows(gated, branch_rows).astype(BF16)
    output_part = output_part.reshape(group // strip, mp, strip, -1)
    pieces = [
        lax.dynamic_index_in_dim(output_part, here ^ m, 1, keepdims=False).reshape(group, -1)
        for m in masks
    ]
    *pieces, d_in = together((*pieces, d_in))
    output_pieces = [swap(pieces[m], m) for m in masks]
    *pieces, hidden = together((*row_product(d_in, w_in, True, parts), hidden))
    feed_pieces = row_product(hidden, w_feed, True, parts, 1)
    output_pieces, pieces, feed_pieces = together((output_pieces, pieces, feed_pieces))
    output_part = jnp.concatenate(by_index(output_pieces), axis=0)
    d_normed_one, output_part = collect(pieces, output_part)
    d_normed_one, feed_pieces = together((d_normed_one, feed_pieces))
    normal_one, factor_one = layer_stats(source)
    d_tokens = d_middle + layer_back(d_normed_one * gain_one, normal_one, factor_one)

    feed_sum, _ = collect(feed_pieces)
    outputs = (middle + feed_sum).astype(BF16)

    width = up_weight.shape[1]
    up_grad = feed_grad[:, :width].astype(F32)
    down_grad = feed_grad[:, width:].astype(F32).T
    output_part, in_grad, d_tokens = together((output_part, in_grad, d_tokens))
    output_grad = scatter(output_part).astype(F32)
    pieces = by_index([in_grad[m * part : (m + 1) * part] for m in masks])
    pieces = by_index([swap(pieces[m], m) for m in masks])
    grads, at = [], 0
    for weight in (query_weight, key_weight, value_weight, gate_weight):
        width = weight.shape[1] // mp
        grads.append(
            jnp.concatenate([p[:, at : at + width] for p in pieces], axis=1).astype(F32)
        )
        at += width

    thin_grads = jnp.stack(
        [
            jnp.sum(d_normed_one * normal_one, axis=0),
            jnp.sum(d_normed_one, axis=0),
            jnp.sum(d_normed_two * normal_two, axis=0),
            jnp.sum(d_normed_two, axis=0),
        ],
        axis=0,
    )
    thin_grads = thin_grads.reshape(4, dp * mp, part).transpose(1, 0, 2).reshape(dp * mp, 4 * part)
    thin_grads = scatter_small(thin_grads).reshape(4, part)
    return (
        outputs,
        d_tokens.astype(BF16),
        *grads,
        output_grad,
        *(thin_grads[n] for n in range(4)),
        up_grad,
        down_grad,
    )


def solution(mesh):
    return jax.shard_map(
        on_device,
        mesh=mesh,
        in_specs=(
            P(("dp", "mp"), None),
            P(("dp", "mp"), None),
            P("dp"),
            P(("dp", "mp"), None),
            P(("dp", "mp"), None),
            P(("dp", "mp"), None),
            P(("dp", "mp"), None),
            P(("dp", "mp"), None),
            P(("dp", "mp")),
            P(("dp", "mp")),
            P(("dp", "mp")),
            P(("dp", "mp")),
            P("dp", "mp"),
            P("mp", "dp"),
        ),
        out_specs=(
            P(("dp", "mp"), None),
            P(("dp", "mp"), None),
            P(("dp", "mp"), None),
            P(("dp", "mp"), None),
            P(("dp", "mp"), None),
            P(("dp", "mp"), None),
            P(("dp", "mp"), None),
            P(("dp", "mp")),
            P(("dp", "mp")),
            P(("dp", "mp")),
            P(("dp", "mp")),
            P("dp", "mp"),
            P("mp", "dp"),
        ),
        check_vma=False,
    )
```
